32 devices in a mesh: dp: 16 (over z, y, x), ep: 2 (over core).
Axes of the slice: x: 2, y: 2, z: 4, core: 2. Of those that a mesh axis runs over, the one named last changes fastest.
Arguments:
- residual: bfloat16 [256, 7168], P(('dp', 'ep')), may hold values from -6 to 6
- queries: bfloat16 [256, 36864], P('dp', 'ep'), may hold values from -57 to 57
- latent_cache: bfloat16 [256, 36864], P('dp'), may hold values from -6 to 6
- lengths: int32 [256], P('dp'), may hold values from 2 to 64, as said below
- destination: int32 [256], replicated, may hold values from 0 to 255, as said below
- w_uv: bfloat16 [64, 512, 128], P('ep'), may hold values from -0.25 to 0.25
- w_o: bfloat16 [8192, 7168], P('ep'), may hold values from -0.0625 to 0.0625
- norm_gain: float32 [7168], replicated, may hold values from 0.1 to 1.9
- experts: int32 [256, 8], P(('dp', 'ep')), may hold values from 0 to 15, all different within a row; in each aligned block of 8 rows (0 to 7, 8 to 15, ...) at most 8 rows name the same one
- gate_weights: float32 [256, 8], P(('dp', 'ep')), may hold values from 0.05 to 0.5
- w_gate: bfloat16 [16, 7168, 1024], P('dp', None, 'ep'), may hold values from -0.0625 to 0.0625
- w_up: bfloat16 [16, 7168, 1024], P('dp', None, 'ep'), may hold values from -0.0625 to 0.0625
- w_down: bfloat16 [16, 1024, 7168], P('dp', 'ep'), may hold values from -0.1875 to 0.1875
Outputs:
- layer_out: bfloat16 [256, 7168], P(('dp', 'ep'))
- arrivals: bfloat16 [64, 36864], P('dp')
The draws below stay inside these ranges and needn't reach their ends.
Inputs may be any that keep to these rules, and one draw needn't show every extreme that they name: `destination`: A permutation. A slot whose entry differs from its index sends its request to a slot of another replica (block of 16 slots); the slots that are left are exactly the slots that are taken. At most 4 requests leave one replica, and in some replica exactly 4. `lengths`: every replica holds a request of length 64. Each row names 8 different experts. Among the rows of one device of dp+ep no expert is named more than 8 times, a bound that some block reaches.
All inputs are finite; a program needn't handle non-finite values.
Results may differ from the reference program's by a relative error of at most 0.0055.
Values may be sent and summed in bfloat16 or wider, within the bound.
No kernel may reach another device: no remote copies, remote signals or barrier semaphores. Data moves between devices by JAX's collectives and lax.ppermute only.
A program may use at most 192 MiB of HBM per device.

```python
import math
import jax
import jax.numpy as jnp
import numpy as np
from jax import lax

D = 7168
HEADS = 64
LAT = 512
KV = 576
V_DIM = 128
MOE_FF = 1024
TOPK = 8
MOVE_MAX = 4
TOK_DEV = 8
CTX = 64
R_DP = 16
REQS = 256
EXPERTS = 16
MOE_CAP = 8
N_DP = 16
N_EP = 2


def moved_plan(key):
    key = jax.random.fold_in(key, 11)
    key_a, key_b, key_c, key_d = jax.random.split(key, 4)
    replicas = jnp.arange(N_DP, dtype=jnp.int32)
    counts = jax.random.randint(key_a, (N_DP,), 0, MOVE_MAX + 1)
    first_full = jax.random.randint(key_b, (), 0, N_DP)
    counts = jnp.where((replicas == first_full) | (replicas == (first_full + 1) % N_DP), MOVE_MAX, counts)
    scores = jax.random.randint(key_c, (N_DP, R_DP), 0, 4096) * R_DP + jnp.arange(R_DP, dtype=jnp.int32)[None, :]
    slot_order = jnp.argsort(scores, axis=1)
    slot_rank = jnp.argsort(slot_order, axis=1)
    moved = (slot_rank < counts[:, None]).reshape(REQS)
    rep_scores = jax.random.randint(key_d, (N_DP,), 0, 4096) * N_DP + replicas
    rep_rank = jnp.argsort(jnp.argsort(rep_scores)).astype(jnp.int32)
    slot_ids = jnp.arange(REQS, dtype=jnp.int32)
    sort_score = jnp.where(moved, rep_rank[slot_ids // R_DP] * REQS + slot_ids, N_DP * REQS + slot_ids)
    listed = jnp.argsort(sort_score).astype(jnp.int32)
    moved_count = jnp.sum(moved.astype(jnp.int32))
    shifted = jnp.where(slot_ids < moved_count, (slot_ids + MOVE_MAX) % jnp.maximum(moved_count, 1), slot_ids)
    return slot_ids.at[listed].set(listed[shifted])


def draw_destination(key, part):
    return moved_plan(key)


def draw_lengths(key, part):
    key = jax.random.fold_in(key, 41)
    key_a, key_b = jax.random.split(key)
    lengths = jax.random.randint(key_a, (REQS,), 2, CTX + 1)
    longest = jax.random.randint(key_b, (N_DP,), 0, R_DP) + jnp.arange(N_DP, dtype=jnp.int32) * R_DP
    return lengths.at[longest].set(CTX)


def draw_latent_cache(key, part):
    key = jax.random.fold_in(key, 31)
    values = jnp.clip(jax.random.normal(key, (REQS, CTX, KV), jnp.float32), -6.0, 6.0)
    return values.reshape(REQS, CTX * KV).astype(jnp.bfloat16)


def draw_queries(key, part):
    key = jax.random.fold_in(key, 37)
    key_a = jax.random.fold_in(key, 0)
    values = jnp.clip(jax.random.normal(key_a, (REQS, HEADS, KV), jnp.float32), -6.0, 6.0)
    return values.reshape(REQS, HEADS * KV).astype(jnp.bfloat16)


def block_scale(stream_key, shape, cuts, low, largest):
    factor_of, own = 1.0, jax.random.fold_in(stream_key, 6)
    for position, blocks in cuts:
        draws = jnp.exp(jax.random.uniform(jax.random.fold_in(own, position), (blocks,), jnp.float32, low / len(cuts), largest / len(cuts)))
        factor_of = factor_of * jnp.repeat(draws, shape[position] // blocks).reshape([-1 if axis == position else 1 for axis in range(len(shape))])
    return factor_of


def shared_out(stream_key, own, number, rows, number_of, top, reach, slope):
    order = jax.random.permutation(stream_key, number_of)
    heavy_load, common = portions_of(number_of, rows * top, reach, slope, True), portions_of(number_of, rows * top, reach, slope, False)
    places = jnp.arange(number_of)

    def named(sizes, offset_by):
        used = int((sizes > 0).sum())
        fixed = max(1, used // 4)
        moved = fixed + (places - fixed + offset_by * (used - fixed)) % max(1, number_of - fixed)
        return jnp.zeros((number_of,), jnp.int32).at[order[jnp.where(places < fixed, places, moved)]].set(jnp.asarray(sizes, jnp.int32))

    sizes = jnp.where(number % 4 == 0, named(heavy_load, number // 4), named(common, number - number // 4 - 1))
    mixed = jax.random.permutation(jax.random.fold_in(own, 3), number_of)
    donor, taker = mixed[0:number_of // 2 * 2:2], mixed[1:number_of // 2 * 2:2]
    room = jnp.minimum(sizes[donor] - 1, reach - sizes[taker]) // 2
    room = jnp.where((donor == order[0]) | (taker == order[0]) | (sizes[taker] == 0), 0, jnp.maximum(room, 0))
    moved = jax.random.randint(jax.random.fold_in(own, 4), (number_of // 2,), 0, 1 << 20) % (room + 1)
    sizes = sizes.at[donor].add(-moved).at[taker].add(moved)
    labels = jnp.searchsorted(jnp.cumsum(sizes), jnp.arange(rows * top), side="right").astype(jnp.int32)
    grid = labels.reshape(top, rows).T
    grid = grid[jax.random.permutation(jax.random.fold_in(own, 1), rows)]
    offset_by = jax.random.randint(jax.random.fold_in(own, 2), (rows, 1), 0, top)
    return jnp.take_along_axis(grid, (jnp.arange(top)[None, :] + offset_by) % top, axis=1)


def portions_of(count, total, limit, skew, full):
    loads = [(1 << 20) // math.isqrt(rank ** skew) + 1 for rank in range(1, count + 1)]
    largest = limit if full else min(limit, max(-(-total // count), total * loads[0] // sum(loads)))
    least = 1 if total - largest >= count - 1 else 0
    holding, rest = [largest] + [least] * (count - 1), total - largest - least * (count - 1)
    while rest > 0:
        free = [i for i in range(1, count) if holding[i] < largest] or [i for i in range(1, count) if holding[i] < limit]
        whole, budget = sum([loads[i] for i in free]), rest
        for i in free:
            addition = min(limit - holding[i], max(1, budget * loads[i] // whole), rest)
            holding[i] = holding[i] + addition
            rest = rest - addition
    return np.array(holding)


def bell_draw(rng, shape, spread, reach, pieces=(), kind=jnp.bfloat16):
    loudness = block_scale(rng, shape, pieces, -0.22, 0.18) if pieces else 1.0
    result = jax.random.normal(rng, shape, jnp.float32) * spread * loudness
    return jnp.minimum(jnp.maximum(result, -reach), reach).astype(kind)


def setup_inputs(seed: int = 0) -> dict:
    key_list = jax.random.split(jax.random.key(seed), 14)
    residual = bell_draw(key_list[0], (REQS, D), 1.0, 6.0, ((0, 32),))
    queries = draw_queries(jax.random.fold_in(key_list[13], 71), 0)
    latent_cache = draw_latent_cache(jax.random.fold_in(key_list[13], 71), 0)
    lengths = draw_lengths(jax.random.fold_in(key_list[13], 71), 0)
    destination = draw_destination(jax.random.fold_in(key_list[13], 71), 0)
    w_uv = bell_draw(key_list[5], (HEADS, LAT, V_DIM), LAT ** -0.5, 0.25, ((0, 2),))
    w_o = bell_draw(key_list[6], (HEADS * V_DIM, D), (HEADS * V_DIM) ** -0.5, 0.0625, ((0, 2),))
    norm_gain = jnp.clip(1.0 + 0.18 * jax.random.normal(key_list[7], (D,), jnp.float32), 0.1, 1.9)
    experts_keys = jax.random.split(jax.random.fold_in(key_list[8], 1), REQS // TOK_DEV)
    experts_turns = jax.random.permutation(jax.random.fold_in(key_list[8], 3), REQS // TOK_DEV)
    experts = jax.vmap(lambda own, number: shared_out(jax.random.fold_in(key_list[8], 2), own, number, TOK_DEV, EXPERTS, TOPK, MOE_CAP, 2))(experts_keys, experts_turns).reshape((REQS, TOPK))
    gate_weights = jnp.clip(jnp.exp(math.log(0.5) - 2.3025851 * jax.random.uniform(key_list[9], (REQS, TOPK), jnp.float32) ** block_scale(key_list[9], (REQS, TOPK), ((0, 32),), -0.2, 0.2)), 0.05, 0.5)
    w_gate = bell_draw(key_list[10], (EXPERTS, D, MOE_FF), D ** -0.5, 0.0625, ((0, 16), (2, 2)))
    w_up = bell_draw(key_list[11], (EXPERTS, D, MOE_FF), D ** -0.5, 0.0625, ((0, 16), (2, 2)))
    w_down = bell_draw(key_list[12], (EXPERTS, MOE_FF, D), MOE_FF ** -0.5, 0.1875, ((0, 16), (1, 2)))
    return dict(residual=residual, queries=queries, latent_cache=latent_cache, lengths=lengths, destination=destination, w_uv=w_uv, w_o=w_o, norm_gain=norm_gain, experts=experts, gate_weights=gate_weights, w_gate=w_gate, w_up=w_up, w_down=w_down)


score_scale = 192.0 ** (-0.5)
norm_eps = 1e-06

def reference(residual, queries, latent_cache, lengths, destination, w_uv, w_o, norm_gain, experts, gate_weights, w_gate, w_up, w_down):
    slot_ids = jnp.arange(REQS, dtype=jnp.int32)
    anchor = jnp.zeros((REQS,), jnp.int32).at[destination].set(slot_ids)
    moved = anchor // R_DP != slot_ids // R_DP
    moved_rank = (jnp.cumsum(moved.reshape(N_DP, R_DP).astype(jnp.int32), axis=1) - 1).reshape(REQS)
    present = latent_cache[anchor]
    targets = jnp.where(moved, slot_ids // R_DP * MOVE_MAX + moved_rank, N_DP * MOVE_MAX).astype(jnp.int32)
    arrivals = jnp.zeros((N_DP * MOVE_MAX + 1, CTX * KV), jnp.bfloat16).at[targets].set(present)[:N_DP * MOVE_MAX]
    latents = present.reshape(REQS, CTX, KV).astype(jnp.float32)
    query_rows = queries.reshape(REQS, HEADS, KV).astype(jnp.float32)
    scores = jnp.einsum('rhk,rtk->rht', query_rows, latents) * score_scale
    in_range = jnp.arange(CTX, dtype=jnp.int32)[None, None, :] < lengths[:, None, None]
    scores = jnp.where(in_range, scores, -jnp.inf)
    row_max = lax.optimization_barrier(jnp.max(scores, axis=2, keepdims=True))
    weights = jnp.where(in_range, jnp.exp(scores - row_max), 0.0)
    prob_rows = (weights / lax.optimization_barrier(jnp.sum(weights, axis=2, keepdims=True))).astype(jnp.bfloat16)
    prob_rows = lax.optimization_barrier(prob_rows).astype(jnp.float32)
    context = jnp.einsum('rht,rtl->rhl', prob_rows, latents[:, :, :LAT]).astype(jnp.bfloat16)
    context = lax.optimization_barrier(context).astype(jnp.float32)
    values = jnp.einsum('rhl,hlv->rhv', context, w_uv.astype(jnp.float32)).astype(jnp.bfloat16)
    attended = jnp.dot(values.reshape(REQS, HEADS * V_DIM), w_o, preferred_element_type=jnp.float32)
    hidden = residual.astype(jnp.float32) + attended
    normed = (hidden * lax.rsqrt(lax.optimization_barrier(jnp.mean(hidden * hidden, axis=1, keepdims=True)) + norm_eps) * norm_gain).astype(jnp.bfloat16)
    block_width = MOE_FF // N_EP

    def one_expert(running, expert_index):
        gate_part = jnp.dot(normed, w_gate[expert_index], preferred_element_type=jnp.float32)
        up_part = jnp.dot(normed, w_up[expert_index], preferred_element_type=jnp.float32)
        activated = (jax.nn.silu(gate_part) * up_part).astype(jnp.bfloat16)
        activated = lax.optimization_barrier(activated).astype(jnp.float32)
        down_blocks = w_down[expert_index].reshape(N_EP, block_width, D).astype(jnp.float32)
        block_outs = jnp.einsum('rbf,bfd->rbd', activated.reshape(REQS, N_EP, block_width), down_blocks).astype(jnp.bfloat16)
        block_outs = lax.optimization_barrier(block_outs).astype(jnp.float32)
        expert_sum = lax.optimization_barrier(jnp.sum(block_outs, axis=1)).astype(jnp.bfloat16)
        expert_sum = lax.optimization_barrier(expert_sum).astype(jnp.float32)
        gate_sum = lax.optimization_barrier(jnp.sum(jnp.where(experts == expert_index, gate_weights, 0.0), axis=1))
        return (running + gate_sum[:, None] * expert_sum, None)
    mixture, unused = lax.scan(one_expert, jnp.zeros((REQS, D), jnp.float32), jnp.arange(EXPERTS, dtype=jnp.int32))
    layer_out = (hidden + mixture).astype(jnp.bfloat16)
    return (layer_out, arrivals)
```

```python
import jax
import jax.numpy as jnp
from jax import lax
from jax.sharding import PartitionSpec as P

LAT = 512
KV = 576
V_DIM = 128
MOVE_MAX = 4
CTX = 64
GATE_COLS = 128


score_scale = 192.0 ** (-0.5)
norm_eps = 1e-06


def flip(x, axis, bit):
    pairs = [(i, i ^ bit) for i in range(lax.axis_size(axis))]
    return lax.ppermute(x, axis, pairs)


def bits_of(axis):
    size = lax.axis_size(axis)
    return [1 << b for b in range(size.bit_length() - 1)]


def expert_rows(flat_rows, w_gate, w_up, w_down):
    gate_part = jnp.dot(flat_rows, w_gate[0], preferred_element_type=jnp.float32)
    up_part = jnp.dot(flat_rows, w_up[0], preferred_element_type=jnp.float32)
    activated = (jax.nn.silu(gate_part) * up_part).astype(jnp.bfloat16)
    return jnp.dot(activated, w_down[0], preferred_element_type=jnp.float32)


def moves(destination, replica_rows):
    slots = destination.shape[0]
    replicas = slots // replica_rows
    ids = jnp.arange(slots, dtype=jnp.int32)
    home = ids // replica_rows
    leaving = destination // replica_rows != home
    earlier = (home[:, None] == home[None, :]) & (ids[:, None] < ids[None, :])
    rank = jnp.sum(jnp.where(earlier & leaving[:, None], 1, 0), axis=0)
    box = jnp.where(leaving, home * MOVE_MAX + rank, -1)
    boxes = jnp.arange(replicas * MOVE_MAX, dtype=jnp.int32)
    to_box = (boxes[:, None] == box[None, :]).astype(jnp.bfloat16)
    lands = (ids[:, None] == destination[None, :]).astype(jnp.bfloat16)
    target = jnp.dot(to_box, lands, preferred_element_type=jnp.float32).astype(jnp.bfloat16)
    picker = lax.dot_general(
        target, to_box, (((1,), (1,)), ((), ())), preferred_element_type=jnp.float32
    ).astype(jnp.bfloat16)
    return to_box, picker


def migrate(packing, picker, latent_cache):
    replicas = lax.axis_size("dp")
    ep_count = lax.axis_size("ep")
    width = latent_cache.shape[1] // ep_count
    share = width // replicas
    own = lax.dynamic_slice_in_dim(latent_cache, lax.axis_index("ep") * width, width, axis=1)
    outbox = jnp.dot(packing, own, preferred_element_type=jnp.float32).astype(jnp.bfloat16)
    outbox = outbox.reshape(MOVE_MAX, replicas, share).transpose(1, 0, 2)
    met = lax.all_to_all(outbox, "dp", split_axis=0, concat_axis=0)
    sorted_rows = jnp.dot(
        picker, met.reshape(replicas * MOVE_MAX, share), preferred_element_type=jnp.float32
    ).astype(jnp.bfloat16)
    taken = lax.all_to_all(
        sorted_rows.reshape(replicas, MOVE_MAX, share), "dp", split_axis=0, concat_axis=0
    )
    part = taken.transpose(1, 0, 2).reshape(MOVE_MAX, width)
    return lax.all_gather(part, "ep", axis=1, tiled=True)


def gather_rows(rows):
    bits = bits_of("dp")
    last = bits[:2]
    held = rows[None]
    for bit in bits[2:]:
        held = jnp.concatenate([held, flip(held, "dp", bit)], axis=0)
    half = rows.shape[1] // 2 // 128 * 128
    parts = [held[:, :, :half], held[:, :, half:]]
    orders = [last[::-1], last]
    for step in range(len(last)):
        parts = [
            jnp.concatenate([part, flip(part, "dp", order[step])], axis=0)
            for part, order in zip(parts, orders)
        ]
    blocks = parts[0].shape[0] // 4
    second = parts[1].reshape((2, 2, blocks) + parts[1].shape[1:])
    parts[1] = jnp.swapaxes(second, 0, 1).reshape(parts[1].shape)
    held = jnp.concatenate(parts, axis=2)
    for bit in bits_of("ep"):
        held = jnp.concatenate([held, flip(held, "ep", bit)], axis=0)
    return held


def add_up(kept, came):
    return (kept.astype(jnp.float32) + came.astype(jnp.float32)).astype(jnp.bfloat16)


def scatter_sums(blocks):
    for bit in bits_of("ep")[::-1]:
        near, far = jnp.split(blocks, 2, axis=0)
        blocks = add_up(near, flip(far, "ep", bit))
    bits = bits_of("dp")
    last = bits[:2]
    half = blocks.shape[2] // 2 // 128 * 128
    parts = [blocks[:, :, :half], blocks[:, :, half:]]
    size = parts[1].shape[0] // 4
    second = parts[1].reshape((2, 2, size) + parts[1].shape[1:])
    parts[1] = jnp.swapaxes(second, 0, 1).reshape(parts[1].shape)
    orders = [last, last[::-1]]
    for step in range(len(last)):
        split = [jnp.split(part, 2, axis=0) for part in parts]
        parts = [
            add_up(near, flip(far, "dp", order[step])) for (near, far), order in zip(split, orders)
        ]
    blocks = jnp.concatenate(parts, axis=2)
    rest = bits[2:]
    for bit in rest[:0:-1]:
        near, far = jnp.split(blocks, 2, axis=0)
        blocks = add_up(near, flip(far, "dp", bit))
    near, far = jnp.split(blocks, 2, axis=0)
    came = flip(far, "dp", rest[0])
    return near[0].astype(jnp.float32) + came[0].astype(jnp.float32)


def head_sums(part):
    if lax.axis_size("ep") != 2:
        return lax.psum_scatter(part, "ep", scatter_dimension=0, tiled=True)
    rows = part.shape[0] // 2
    own = lax.axis_index("ep")
    mine = lax.dynamic_slice_in_dim(part, own * rows, rows)
    other = lax.dynamic_slice_in_dim(part, (1 - own) * rows, rows)
    return mine + flip(other, "ep", 1)


def per_device(
    residual,
    queries,
    latent_cache,
    lengths,
    destination,
    w_uv,
    w_o,
    norm_gain,
    experts,
    gate_weights,
    w_gate,
    w_up,
    w_down,
):
    replica_rows = latent_cache.shape[0]
    replicas = destination.shape[0] // replica_rows
    own_replica = lax.axis_index("dp")
    to_box, picker = moves(destination, replica_rows)
    packing = lax.dynamic_slice(
        to_box, (own_replica * MOVE_MAX, own_replica * replica_rows), (MOVE_MAX, replica_rows)
    )
    arrivals = migrate(packing, picker, latent_cache)
    own_leave = jnp.sum(packing.astype(jnp.float32), axis=0) > 0
    fetched = lax.dot_general(
        packing, arrivals, (((0,), (0,)), ((), ())), preferred_element_type=jnp.float32
    ).astype(jnp.bfloat16)
    present = jnp.where(own_leave[:, None], fetched, latent_cache)
    heads_dev = w_uv.shape[0]
    latents = present.reshape(replica_rows, CTX, KV)
    query_rows = queries.reshape(replica_rows, heads_dev, KV)
    scores = (
        jnp.einsum("rhk,rtk->rht", query_rows, latents, preferred_element_type=jnp.float32)
        * score_scale
    )
    in_range = jnp.arange(CTX, dtype=jnp.int32)[None, None, :] < lengths[:, None, None]
    scores = jnp.where(in_range, scores, -jnp.inf)
    row_max = jnp.max(scores, axis=2, keepdims=True)
    weights = jnp.where(in_range, jnp.exp(scores - row_max), 0.0)
    prob_rows = (weights / jnp.sum(weights, axis=2, keepdims=True)).astype(jnp.bfloat16)
    context = jnp.einsum(
        "rht,rtl->rhl", prob_rows, latents[:, :, :LAT], preferred_element_type=jnp.float32
    ).astype(jnp.bfloat16)
    values = jnp.einsum("rhl,hlv->rhv", context, w_uv, preferred_element_type=jnp.float32).astype(
        jnp.bfloat16
    )
    values = values.reshape(replica_rows, heads_dev * V_DIM)
    width = residual.shape[1]
    attended = head_sums(jnp.dot(values, w_o, preferred_element_type=jnp.float32))
    hidden = residual.astype(jnp.float32) + attended
    normed = (
        hidden * lax.rsqrt(jnp.mean(hidden * hidden, axis=1, keepdims=True) + norm_eps) * norm_gain
    ).astype(jnp.bfloat16)
    expert_ids = jnp.arange(replicas, dtype=jnp.int32)
    matches = experts[:, :, None] == expert_ids[None, None, :]
    gate_sum = jnp.sum(jnp.where(matches, gate_weights[:, :, None], 0.0), axis=1)
    terms = []
    left = gate_sum
    for _ in range(3):
        term = lax.reduce_precision(left, 8, 7)
        terms.append(term.astype(jnp.bfloat16))
        left = left - term
    terms.append(jnp.zeros((gate_sum.shape[0], GATE_COLS - 3 * replicas), jnp.bfloat16))
    gathered = gather_rows(jnp.concatenate([normed] + terms, axis=1))
    flat = gathered.reshape(-1, width + GATE_COLS)
    chosen = (jnp.arange(GATE_COLS, dtype=jnp.int32) % replicas == own_replica).astype(jnp.float32)
    gates = jnp.sum(flat[:, width:].astype(jnp.float32) * chosen[None, :], axis=1)
    served = expert_rows(flat[:, :width], w_gate, w_up, w_down) * gates[:, None]
    mixture = scatter_sums(served.astype(jnp.bfloat16).reshape(gathered.shape[:2] + (width,)))
    layer_out = (hidden + mixture).astype(jnp.bfloat16)
    return (layer_out, arrivals)


def solution(mesh):
    in_specs = (
        P(("dp", "ep"), None),
        P("dp", "ep"),
        P("dp", None),
        P("dp"),
        P(),
        P("ep", None, None),
        P("ep", None),
        P(),
        P(("dp", "ep"), None),
        P(("dp", "ep"), None),
        P("dp", None, "ep"),
        P("dp", None, "ep"),
        P("dp", "ep", None),
    )
    out_specs = (P(("dp", "ep"), None), P("dp", None))
    return jax.shard_map(
        per_device, mesh=mesh, in_specs=in_specs, out_specs=out_specs, check_vma=False
    )
```

```python
import functools

import jax
import jax.numpy as jnp
from jax import lax
from jax.experimental import pallas as pl
from jax.experimental.pallas import tpu as pltpu
from jax.sharding import PartitionSpec as P

LAT = 512
KV = 576
V_DIM = 128
MOVE_MAX = 4
CTX = 64
GATE_COLS = 128


score_scale = 192.0 ** (-0.5)
norm_eps = 1e-06


def flip(x, axis, bit):
    pairs = [(i, i ^ bit) for i in range(lax.axis_size(axis))]
    return lax.ppermute(x, axis, pairs)


def bits_of(axis):
    size = lax.axis_size(axis)
    return [1 << b for b in range(size.bit_length() - 1)]


CHUNKS = 4


def read_rows(sets, width, half, at, size):
    parts = []
    for own, near_x, near_y, low, high in sets:
        for ref in (own, near_x, near_y):
            parts.append(ref[:, pl.ds(at, size)])
        if half == 0:
            parts.append(low[:, pl.ds(at, size)])
        else:
            parts.append(high[:, pl.ds(pl.multiple_of(at - width // 2, 128), size)])
    return jnp.concatenate(parts, axis=0)


def expert_kernel(set_count, *refs):
    flat, refs = refs[: 5 * set_count], refs[5 * set_count :]
    sets = [flat[5 * n : 5 * n + 5] for n in range(set_count)]
    mask, w_gate, w_up, w_down, far, kept, gate_buf, up_buf, down_buf, gate_acc, up_acc, act, sems = refs
    width = w_gate.shape[1]
    size = width // CHUNKS
    half_rows = far.shape[0]

    def span(n):
        return pl.ds(pl.multiple_of(n * size, size), size)

    def copies_in(n):
        return (
            pltpu.make_async_copy(w_gate.at[0, span(n)], gate_buf.at[n], sems.at[0, n]),
            pltpu.make_async_copy(w_up.at[0, span(n)], up_buf.at[n], sems.at[1, n]),
        )

    def copy_down(n):
        return pltpu.make_async_copy(w_down.at[0, :, span(n)], down_buf.at[n], sems.at[2, n])

    for n in range(CHUNKS):
        for copy in copies_in(n):
            copy.start()
    for n in range(CHUNKS):
        copy_down(n).start()
    gate_acc[...] = jnp.zeros_like(gate_acc)
    up_acc[...] = jnp.zeros_like(up_acc)
    for half in range(2):

        @pl.loop(half * CHUNKS // 2, (half + 1) * CHUNKS // 2)
        def _(n):
            for copy in copies_in(n):
                copy.wait()
            rows = read_rows(sets, width, half, pl.multiple_of(n * size, size), size)
            gate_acc[...] += jnp.dot(rows, gate_buf[n], preferred_element_type=jnp.float32)
            up_acc[...] += jnp.dot(rows, up_buf[n], preferred_element_type=jnp.float32)

    tails = []
    for own, near_x, near_y, low, high in sets:
        tails += [ref[:, width:] for ref in (own, near_x, near_y)] + [high[:, width // 2 :]]
    terms = jnp.concatenate(tails, axis=0).astype(jnp.float32)
    gates = jnp.sum(terms * mask[...], axis=1, keepdims=True)
    gated = gate_acc[...]
    act[...] = (gated / (1.0 + jnp.exp(-gated)) * up_acc[...] * gates).astype(jnp.bfloat16)
    kept[...] = act[:half_rows]

    @pl.loop(0, CHUNKS)
    def _(n):
        copy_down(n).wait()
        far[:, span(n)] = jnp.dot(
            act[half_rows:], down_buf[n], preferred_element_type=jnp.float32
        ).astype(jnp.bfloat16)


def vmem_spec():
    return pl.BlockSpec(memory_space=pltpu.VMEM)


def experts_far(sets, mask, w_gate, w_up, w_down):
    width, hidden_units = w_gate.shape[1:]
    rows = sum(piece.shape[0] for pieces in sets for piece in pieces[:4])
    size = width // CHUNKS
    flat = [piece for pieces in sets for piece in pieces]
    return pl.pallas_call(
        functools.partial(expert_kernel, len(sets)),
        out_shape=(
            jax.ShapeDtypeStruct((rows // 2, width), jnp.bfloat16),
            jax.ShapeDtypeStruct((rows // 2, hidden_units), jnp.bfloat16),
        ),
        in_specs=[vmem_spec()] * (len(flat) + 1) + [pl.BlockSpec(memory_space=pl.ANY)] * 3,
        out_specs=(vmem_spec(), vmem_spec()),
        scratch_shapes=[
            pltpu.VMEM((CHUNKS, size, hidden_units), jnp.bfloat16),
            pltpu.VMEM((CHUNKS, size, hidden_units), jnp.bfloat16),
            pltpu.VMEM((CHUNKS, hidden_units, size), jnp.bfloat16),
            pltpu.VMEM((rows, hidden_units), jnp.float32),
            pltpu.VMEM((rows, hidden_units), jnp.float32),
            pltpu.VMEM((rows, hidden_units), jnp.bfloat16),
            pltpu.SemaphoreType.DMA((3, CHUNKS)),
        ],
        compiler_params=pltpu.CompilerParams(vmem_limit_bytes=48 << 20),
        cost_estimate=pl.CostEstimate(
            flops=5 * rows * width * hidden_units,
            bytes_accessed=6 * width * hidden_units + 3 * rows * width,
            transcendentals=rows * hidden_units,
        ),
        name="experts_far",
    )(*flat, mask, w_gate, w_up, w_down)


def down_kernel(kept, w_down, near, down_buf, sems):
    size = down_buf.shape[2]

    def copy(n):
        columns = pl.ds(pl.multiple_of(n * size, size), size)
        return pltpu.make_async_copy(w_down.at[0, :, columns], down_buf.at[n], sems.at[n])

    for n in range(CHUNKS):
        copy(n).start()

    @pl.loop(0, CHUNKS)
    def _(n):
        copy(n).wait()
        columns = pl.ds(pl.multiple_of(n * size, size), size)
        near[:, columns] = jnp.dot(
            kept[...], down_buf[n], preferred_element_type=jnp.float32
        ).astype(jnp.bfloat16)


def experts_near(kept, w_down):
    rows, hidden_units = kept.shape
    width = w_down.shape[2]
    size = width // CHUNKS
    return pl.pallas_call(
        down_kernel,
        out_shape=jax.ShapeDtypeStruct((rows, width), jnp.bfloat16),
        in_specs=[vmem_spec(), pl.BlockSpec(memory_space=pl.ANY)],
        out_specs=vmem_spec(),
        scratch_shapes=[
            pltpu.VMEM((CHUNKS, hidden_units, size), jnp.bfloat16),
            pltpu.SemaphoreType.DMA((CHUNKS,)),
        ],
        compiler_params=pltpu.CompilerParams(vmem_limit_bytes=32 << 20),
        cost_estimate=pl.CostEstimate(
            flops=2 * rows * width * hidden_units,
            bytes_accessed=2 * width * hidden_units + 2 * rows * width,
            transcendentals=0,
        ),
        name="experts_near",
    )(kept, w_down)


def moves(destination, replica_rows):
    slots = destination.shape[0]
    replicas = slots // replica_rows
    ids = jnp.arange(slots, dtype=jnp.int32)
    home = ids // replica_rows
    leaving = destination // replica_rows != home
    earlier = (home[:, None] == home[None, :]) & (ids[:, None] < ids[None, :])
    rank = jnp.sum(jnp.where(earlier & leaving[:, None], 1, 0), axis=0)
    box = jnp.where(leaving, home * MOVE_MAX + rank, -1)
    boxes = jnp.arange(replicas * MOVE_MAX, dtype=jnp.int32)
    to_box = (boxes[:, None] == box[None, :]).astype(jnp.bfloat16)
    lands = (ids[:, None] == destination[None, :]).astype(jnp.bfloat16)
    target = jnp.dot(to_box, lands, preferred_element_type=jnp.float32).astype(jnp.bfloat16)
    picker = lax.dot_general(
        target, to_box, (((1,), (1,)), ((), ())), preferred_element_type=jnp.float32
    ).astype(jnp.bfloat16)
    return to_box, picker


def migrate(packing, picker, latent_cache):
    replicas = lax.axis_size("dp")
    ep_count = lax.axis_size("ep")
    width = latent_cache.shape[1] // ep_count
    share = width // replicas
    own = lax.dynamic_slice_in_dim(latent_cache, lax.axis_index("ep") * width, width, axis=1)
    outbox = jnp.dot(packing, own, preferred_element_type=jnp.float32).astype(jnp.bfloat16)
    outbox = outbox.reshape(MOVE_MAX, replicas, share).transpose(1, 0, 2)
    met = lax.all_to_all(outbox, "dp", split_axis=0, concat_axis=0)
    sorted_rows = jnp.dot(
        picker, met.reshape(replicas * MOVE_MAX, share), preferred_element_type=jnp.float32
    ).astype(jnp.bfloat16)
    taken = lax.all_to_all(
        sorted_rows.reshape(replicas, MOVE_MAX, share), "dp", split_axis=0, concat_axis=0
    )
    part = taken.transpose(1, 0, 2).reshape(MOVE_MAX, width)
    return lax.all_gather(part, "ep", axis=1, tiled=True)


def gather_rows(rows):
    inner_x, inner_y, *outer = bits_of("dp")
    for bit in outer:
        rows = jnp.concatenate([rows, flip(rows, "dp", bit)], axis=0)
    half = rows.shape[1] // 2 // 128 * 128
    near_x = flip(rows, "dp", inner_x)
    near_y = flip(rows, "dp", inner_y)
    low = flip(near_y[:, :half], "dp", inner_x)
    high = flip(near_x[:, half:], "dp", inner_y)
    sets = [(rows, near_x, near_y, low, high)]
    for bit in bits_of("ep"):
        sets = sets + [tuple(flip(piece, "ep", bit) for piece in pieces) for pieces in sets]
    return sets


def plus(*terms):
    return sum(term.astype(jnp.float32) for term in terms)


def narrow(x):
    return x.astype(jnp.bfloat16)


def scatter_sums(near, far):
    bits = bits_of("ep")[::-1]
    for bit in bits:
        came = flip(far, "ep", bit)
        if bit != bits[-1]:
            both = narrow(plus(near, came))
            near, far = jnp.split(both, 2, axis=0)
    inner_x, inner_y, *outer = bits_of("dp")
    width = near.shape[1]
    half = width // 2
    near = jnp.split(near, 4, axis=0)
    came = jnp.split(came, 4, axis=0)
    diagonal = narrow(plus(near[3], came[3]))
    low = flip(diagonal[:, :half], "dp", inner_x)
    high = flip(diagonal[:, half:], "dp", inner_y)
    to_x = plus(near[1], came[1])
    to_y = plus(near[2], came[2])
    to_x = narrow(jnp.concatenate([to_x[:, :half], to_x[:, half:] + plus(high)], axis=1))
    to_y = narrow(jnp.concatenate([to_y[:, :half] + plus(low), to_y[:, half:]], axis=1))
    from_x = flip(to_x, "dp", inner_x)
    from_y = flip(to_y, "dp", inner_y)
    total = plus(near[0], came[0], from_x, from_y)
    for bit in outer[::-1]:
        mine, other = jnp.split(total, 2, axis=0)
        total = mine + plus(flip(narrow(other), "dp", bit))
    return total


def head_sums(part):
    if lax.axis_size("ep") != 2:
        return lax.psum_scatter(part, "ep", scatter_dimension=0, tiled=True)
    rows = part.shape[0] // 2
    own = lax.axis_index("ep")
    mine = lax.dynamic_slice_in_dim(part, own * rows, rows)
    other = lax.dynamic_slice_in_dim(part, (1 - own) * rows, rows)
    return mine + flip(other, "ep", 1)


def per_device(
    residual,
    queries,
    latent_cache,
    lengths,
    destination,
    w_uv,
    w_o,
    norm_gain,
    experts,
    gate_weights,
    w_gate,
    w_up,
    w_down,
):
    replica_rows = latent_cache.shape[0]
    replicas = destination.shape[0] // replica_rows
    own_replica = lax.axis_index("dp")
    to_box, picker = moves(destination, replica_rows)
    packing = lax.dynamic_slice(
        to_box, (own_replica * MOVE_MAX, own_replica * replica_rows), (MOVE_MAX, replica_rows)
    )
    arrivals = migrate(packing, picker, latent_cache)
    own_leave = jnp.sum(packing.astype(jnp.float32), axis=0) > 0
    fetched = lax.dot_general(
        packing, arrivals, (((0,), (0,)), ((), ())), preferred_element_type=jnp.float32
    ).astype(jnp.bfloat16)
    present = jnp.where(own_leave[:, None], fetched, latent_cache)
    heads_dev = w_uv.shape[0]
    latents = present.reshape(replica_rows, CTX, KV)
    query_rows = queries.reshape(replica_rows, heads_dev, KV)
    scores = (
        jnp.einsum("rhk,rtk->rht", query_rows, latents, preferred_element_type=jnp.float32)
        * score_scale
    )
    in_range = jnp.arange(CTX, dtype=jnp.int32)[None, None, :] < lengths[:, None, None]
    scores = jnp.where(in_range, scores, -jnp.inf)
    row_max = jnp.max(scores, axis=2, keepdims=True)
    weights = jnp.where(in_range, jnp.exp(scores - row_max), 0.0)
    prob_rows = (weights / jnp.sum(weights, axis=2, keepdims=True)).astype(jnp.bfloat16)
    context = jnp.einsum(
        "rht,rtl->rhl", prob_rows, latents[:, :, :LAT], preferred_element_type=jnp.float32
    ).astype(jnp.bfloat16)
    values = jnp.einsum("rhl,hlv->rhv", context, w_uv, preferred_element_type=jnp.float32).astype(
        jnp.bfloat16
    )
    values = values.reshape(replica_rows, heads_dev * V_DIM)
    width = residual.shape[1]
    attended = head_sums(jnp.dot(values, w_o, preferred_element_type=jnp.float32))
    hidden = residual.astype(jnp.float32) + attended
    normed = (
        hidden * lax.rsqrt(jnp.mean(hidden * hidden, axis=1, keepdims=True) + norm_eps) * norm_gain
    ).astype(jnp.bfloat16)
    expert_ids = jnp.arange(replicas, dtype=jnp.int32)
    matches = experts[:, :, None] == expert_ids[None, None, :]
    gate_sum = jnp.sum(jnp.where(matches, gate_weights[:, :, None], 0.0), axis=1)
    terms = []
    left = gate_sum
    for _ in range(3):
        term = lax.reduce_precision(left, 8, 7)
        terms.append(term.astype(jnp.bfloat16))
        left = left - term
    terms.append(jnp.zeros((gate_sum.shape[0], GATE_COLS - 3 * replicas), jnp.bfloat16))
    sets = gather_rows(jnp.concatenate([normed] + terms, axis=1))
    columns = jnp.arange(GATE_COLS, dtype=jnp.int32)[None, :]
    chosen = (columns < 3 * replicas) & (columns % replicas == own_replica)
    far, kept = experts_far(sets, chosen.astype(jnp.float32), w_gate, w_up, w_down)
    mixture = scatter_sums(experts_near(kept, w_down), far)
    layer_out = (hidden + mixture).astype(jnp.bfloat16)
    return (layer_out, arrivals)


def solution(mesh):
    in_specs = (
        P(("dp", "ep"), None),
        P("dp", "ep"),
        P("dp", None),
        P("dp"),
        P(),
        P("ep", None, None),
        P("ep", None),
        P(),
        P(("dp", "ep"), None),
        P(("dp", "ep"), None),
        P("dp", None, "ep"),
        P("dp", None, "ep"),
        P("dp", "ep", None),
    )
    out_specs = (P(("dp", "ep"), None), P("dp", None))
    return jax.shard_map(
        per_device, mesh=mesh, in_specs=in_specs, out_specs=out_specs, check_vma=False
    )
```

```python
import functools

import jax
import jax.numpy as jnp
from jax import lax
from jax.experimental import pallas as pl
from jax.experimental.pallas import tpu as pltpu
from jax.sharding import PartitionSpec as P

LAT = 512
KV = 576
V_DIM = 128
MOVE_MAX = 4
CTX = 64
GATE_COLS = 128


score_scale = 192.0 ** (-0.5)
norm_eps = 1e-06


def flip(x, axis, bit):
    pairs = [(i, i ^ bit) for i in range(lax.axis_size(axis))]
    return lax.ppermute(x, axis, pairs)


def bits_of(axis):
    size = lax.axis_size(axis)
    return [1 << b for b in range(size.bit_length() - 1)]


CHUNKS = 4


def vmem_spec():
    return pl.BlockSpec(memory_space=pltpu.VMEM)


def any_spec():
    return pl.BlockSpec(memory_space=pl.ANY)


def span(n, size):
    return pl.ds(pl.multiple_of(n * size, size), size)


def values_kernel(context, w_uv, w_o, part, values, uv_buf, o_buf, uv_sems, o_sems):
    heads, _, dim = w_uv.shape
    groups = uv_sems.shape[0]
    step = heads // groups
    chunks, depth, width = o_buf.shape

    def copy_uv(g):
        own = pl.ds(g * step, step)
        return pltpu.make_async_copy(w_uv.at[own], uv_buf.at[own], uv_sems.at[g])

    def copy_o(n):
        rows = pl.ds(n * depth, depth)
        return pltpu.make_async_copy(w_o.at[rows, pl.ds(0, width)], o_buf.at[n], o_sems.at[n])

    for g in range(groups):
        copy_uv(g).start()
    for n in range(chunks):
        copy_o(n).start()
    for g in range(groups):
        copy_uv(g).wait()
        for h in range(g * step, (g + 1) * step):
            values[:, h * dim : (h + 1) * dim] = jnp.dot(
                context[h], uv_buf[h], preferred_element_type=jnp.float32
            ).astype(jnp.bfloat16)
    for n in range(chunks):
        copy_o(n).wait()
        product = jnp.dot(
            values[:, n * depth : (n + 1) * depth], o_buf[n], preferred_element_type=jnp.float32
        )
        if n == 0:
            part[...] = product
        else:
            part[...] += product


def values_and_first(context, w_uv, w_o, width):
    heads, rows, latent = context.shape
    depth = w_o.shape[0]
    chunks = 8
    groups = 4 if heads % 4 == 0 else 1
    return pl.pallas_call(
        values_kernel,
        out_shape=(
            jax.ShapeDtypeStruct((rows, width), jnp.float32),
            jax.ShapeDtypeStruct((rows, depth), jnp.bfloat16),
        ),
        in_specs=[vmem_spec(), any_spec(), any_spec()],
        out_specs=(vmem_spec(), vmem_spec()),
        scratch_shapes=[
            pltpu.VMEM(w_uv.shape, jnp.bfloat16),
            pltpu.VMEM((chunks, depth // chunks, width), jnp.bfloat16),
            pltpu.SemaphoreType.DMA((groups,)),
            pltpu.SemaphoreType.DMA((chunks,)),
        ],
        compiler_params=pltpu.CompilerParams(vmem_limit_bytes=44 << 20),
        cost_estimate=pl.CostEstimate(
            flops=2 * rows * depth * (width + latent),
            bytes_accessed=2 * depth * (width + latent),
            transcendentals=0,
        ),
        name="values_and_first",
    )(context, w_uv, w_o)


def columns_kernel(start, values, w_o, part, o_buf, o_sems):
    chunks, depth, width = o_buf.shape

    def copy_o(n):
        rows = pl.ds(n * depth, depth)
        return pltpu.make_async_copy(w_o.at[rows, pl.ds(start, width)], o_buf.at[n], o_sems.at[n])

    for n in range(chunks):
        copy_o(n).start()
    for n in range(chunks):
        copy_o(n).wait()
        product = jnp.dot(
            values[:, n * depth : (n + 1) * depth], o_buf[n], preferred_element_type=jnp.float32
        )
        if n == 0:
            part[...] = product
        else:
            part[...] += product


def more_columns(values, w_o, start, width):
    rows, depth = values.shape
    chunks = 8
    return pl.pallas_call(
        functools.partial(columns_kernel, start),
        out_shape=jax.ShapeDtypeStruct((rows, width), jnp.float32),
        in_specs=[vmem_spec(), any_spec()],
        out_specs=vmem_spec(),
        scratch_shapes=[
            pltpu.VMEM((chunks, depth // chunks, width), jnp.bfloat16),
            pltpu.SemaphoreType.DMA((chunks,)),
        ],
        compiler_params=pltpu.CompilerParams(vmem_limit_bytes=24 << 20),
        cost_estimate=pl.CostEstimate(
            flops=2 * rows * depth * width, bytes_accessed=2 * depth * width, transcendentals=0
        ),
        name="more_columns",
    )(values, w_o)


def first_kernel(set_count, *refs):
    flat, refs = refs[: 4 * set_count], refs[4 * set_count :]
    w_gate, w_up, gate_acc, up_acc, gate_buf, up_buf, sems = refs
    chunks, size, _ = gate_buf.shape

    def copies_in(n):
        return (
            pltpu.make_async_copy(w_gate.at[0, span(n, size)], gate_buf.at[n], sems.at[0, n]),
            pltpu.make_async_copy(w_up.at[0, span(n, size)], up_buf.at[n], sems.at[1, n]),
        )

    for n in range(chunks):
        for copy in copies_in(n):
            copy.start()
    gate_acc[...] = jnp.zeros_like(gate_acc)
    up_acc[...] = jnp.zeros_like(up_acc)

    @pl.loop(0, chunks)
    def _(n):
        for copy in copies_in(n):
            copy.wait()
        rows = jnp.concatenate([ref[:, span(n, size)] for ref in flat], axis=0)
        gate_acc[...] += jnp.dot(rows, gate_buf[n], preferred_element_type=jnp.float32)
        up_acc[...] += jnp.dot(rows, up_buf[n], preferred_element_type=jnp.float32)


def experts_first(sets, w_gate, w_up):
    width, hidden_units = w_gate.shape[1:]
    size = width // CHUNKS
    flat = [piece for pieces in sets for piece in pieces]
    rows = sum(piece.shape[0] for piece in flat)
    sums = jax.ShapeDtypeStruct((rows, hidden_units), jnp.float32)
    return pl.pallas_call(
        functools.partial(first_kernel, len(sets)),
        out_shape=(sums, sums),
        in_specs=[vmem_spec()] * len(flat) + [any_spec()] * 2,
        out_specs=(vmem_spec(), vmem_spec()),
        scratch_shapes=[
            pltpu.VMEM((CHUNKS // 2, size, hidden_units), jnp.bfloat16),
            pltpu.VMEM((CHUNKS // 2, size, hidden_units), jnp.bfloat16),
            pltpu.SemaphoreType.DMA((2, CHUNKS // 2)),
        ],
        compiler_params=pltpu.CompilerParams(vmem_limit_bytes=32 << 20),
        cost_estimate=pl.CostEstimate(
            flops=2 * rows * width * hidden_units,
            bytes_accessed=2 * width * hidden_units + rows * width,
            transcendentals=0,
        ),
        name="experts_first",
    )(*flat, w_gate, w_up)


def far_kernel(set_count, *refs):
    flat, refs = refs[: 5 * set_count], refs[5 * set_count :]
    sets = [flat[5 * n : 5 * n + 5] for n in range(set_count)]
    mask, gate_first, up_first, w_gate, w_up, w_down, far, kept = refs[:8]
    gate_buf, up_buf, down_buf, gate_acc, up_acc, act, sems = refs[8:]
    chunks, size, _ = gate_buf.shape
    half = w_gate.shape[1] // 2
    half_rows = far.shape[0]

    def copies_in(n):
        rows = pl.ds(half + n * size, size)
        return (
            pltpu.make_async_copy(w_gate.at[0, rows], gate_buf.at[n], sems.at[0, n]),
            pltpu.make_async_copy(w_up.at[0, rows], up_buf.at[n], sems.at[1, n]),
        )

    def copy_down(n):
        return pltpu.make_async_copy(w_down.at[0, :, span(n, size)], down_buf.at[n], sems.at[2, n])

    for n in range(chunks):
        for copy in copies_in(n):
            copy.start()
    for n in range(CHUNKS):
        copy_down(n).start()
    tails = []
    for own, near_x, near_y, low, high in sets:
        tails += [ref[:, half:] for ref in (own, near_x, near_y)] + [high[:, size:]]
    terms = jnp.concatenate(tails, axis=0).astype(jnp.float32)
    gates = jnp.sum(terms * mask[0:1], axis=1, keepdims=True)
    factors = jnp.sum(terms * mask[1:2], axis=1, keepdims=True)
    for n in range(chunks):
        parts = []
        for own, near_x, near_y, low, high in sets:
            parts += [ref[:, n * size : (n + 1) * size] for ref in (own, near_x, near_y)]
            parts.append((low, high)[n][:, :size])
        rows = jnp.concatenate(parts, axis=0)
        for copy in copies_in(n):
            copy.wait()
        before = (gate_first, up_first) if n == 0 else (gate_acc, up_acc)
        gate_acc[...] = before[0][...] + jnp.dot(
            rows, gate_buf[n], preferred_element_type=jnp.float32
        )
        up_acc[...] = before[1][...] + jnp.dot(rows, up_buf[n], preferred_element_type=jnp.float32)
    gated = gate_acc[...] * factors
    raised = up_acc[...] * factors
    act[...] = (gated / (1.0 + jnp.exp(-gated)) * raised * gates).astype(jnp.bfloat16)
    kept[...] = act[:half_rows]

    @pl.loop(0, CHUNKS)
    def _(n):
        copy_down(n).wait()
        far[:, span(n, size)] = jnp.dot(
            act[half_rows:], down_buf[n], preferred_element_type=jnp.float32
        ).astype(jnp.bfloat16)


def experts_far(sets, mask, sums, w_gate, w_up, w_down):
    width, hidden_units = w_gate.shape[1:]
    rows = sums[0].shape[0]
    size = width // CHUNKS
    flat = [piece for pieces in sets for piece in pieces]
    return pl.pallas_call(
        functools.partial(far_kernel, len(sets)),
        out_shape=(
            jax.ShapeDtypeStruct((rows // 2, width), jnp.bfloat16),
            jax.ShapeDtypeStruct((rows // 2, hidden_units), jnp.bfloat16),
        ),
        in_specs=[vmem_spec()] * (len(flat) + 3) + [any_spec()] * 3,
        out_specs=(vmem_spec(), vmem_spec()),
        scratch_shapes=[
            pltpu.VMEM((CHUNKS // 2, size, hidden_units), jnp.bfloat16),
            pltpu.VMEM((CHUNKS // 2, size, hidden_units), jnp.bfloat16),
            pltpu.VMEM((CHUNKS, hidden_units, size), jnp.bfloat16),
            pltpu.VMEM((rows, hidden_units), jnp.float32),
            pltpu.VMEM((rows, hidden_units), jnp.float32),
            pltpu.VMEM((rows, hidden_units), jnp.bfloat16),
            pltpu.SemaphoreType.DMA((3, CHUNKS)),
        ],
        compiler_params=pltpu.CompilerParams(vmem_limit_bytes=48 << 20),
        cost_estimate=pl.CostEstimate(
            flops=3 * rows * width * hidden_units,
            bytes_accessed=4 * width * hidden_units + 3 * rows * width,
            transcendentals=rows * hidden_units,
        ),
        name="experts_far",
    )(*flat, mask, *sums, w_gate, w_up, w_down)


def down_kernel(kept, w_down, near, down_buf, sems):
    size = down_buf.shape[2]

    def copy(n):
        columns = pl.ds(pl.multiple_of(n * size, size), size)
        return pltpu.make_async_copy(w_down.at[0, :, columns], down_buf.at[n], sems.at[n])

    for n in range(CHUNKS):
        copy(n).start()

    @pl.loop(0, CHUNKS)
    def _(n):
        copy(n).wait()
        columns = pl.ds(pl.multiple_of(n * size, size), size)
        near[:, columns] = jnp.dot(
            kept[...], down_buf[n], preferred_element_type=jnp.float32
        ).astype(jnp.bfloat16)


def experts_near(kept, w_down):
    rows, hidden_units = kept.shape
    width = w_down.shape[2]
    size = width // CHUNKS
    return pl.pallas_call(
        down_kernel,
        out_shape=jax.ShapeDtypeStruct((rows, width), jnp.bfloat16),
        in_specs=[vmem_spec(), any_spec()],
        out_specs=vmem_spec(),
        scratch_shapes=[
            pltpu.VMEM((CHUNKS, hidden_units, size), jnp.bfloat16),
            pltpu.SemaphoreType.DMA((CHUNKS,)),
        ],
        compiler_params=pltpu.CompilerParams(vmem_limit_bytes=32 << 20),
        cost_estimate=pl.CostEstimate(
            flops=2 * rows * width * hidden_units,
            bytes_accessed=2 * width * hidden_units + 2 * rows * width,
            transcendentals=0,
        ),
        name="experts_near",
    )(kept, w_down)


def moves(destination, replica_rows):
    slots = destination.shape[0]
    replicas = slots // replica_rows
    ids = jnp.arange(slots, dtype=jnp.int32)
    home = ids // replica_rows
    leaving = destination // replica_rows != home
    earlier = (home[:, None] == home[None, :]) & (ids[:, None] < ids[None, :])
    rank = jnp.sum(jnp.where(earlier & leaving[:, None], 1, 0), axis=0)
    box = jnp.where(leaving, home * MOVE_MAX + rank, -1)
    boxes = jnp.arange(replicas * MOVE_MAX, dtype=jnp.int32)
    to_box = (boxes[:, None] == box[None, :]).astype(jnp.bfloat16)
    lands = (ids[:, None] == destination[None, :]).astype(jnp.bfloat16)
    target = jnp.dot(to_box, lands, preferred_element_type=jnp.float32).astype(jnp.bfloat16)
    picker = lax.dot_general(
        target, to_box, (((1,), (1,)), ((), ())), preferred_element_type=jnp.float32
    ).astype(jnp.bfloat16)
    return to_box, picker


def migrate(packing, picker, latent_cache):
    replicas = lax.axis_size("dp")
    ep_count = lax.axis_size("ep")
    width = latent_cache.shape[1] // ep_count
    share = width // replicas
    own = lax.dynamic_slice_in_dim(latent_cache, lax.axis_index("ep") * width, width, axis=1)
    outbox = jnp.dot(packing, own, preferred_element_type=jnp.float32).astype(jnp.bfloat16)
    outbox = outbox.reshape(MOVE_MAX, replicas, share).transpose(1, 0, 2)
    met = lax.all_to_all(outbox, "dp", split_axis=0, concat_axis=0)
    sorted_rows = jnp.dot(
        picker, met.reshape(replicas * MOVE_MAX, share), preferred_element_type=jnp.float32
    ).astype(jnp.bfloat16)
    taken = lax.all_to_all(
        sorted_rows.reshape(replicas, MOVE_MAX, share), "dp", split_axis=0, concat_axis=0
    )
    part = taken.transpose(1, 0, 2).reshape(MOVE_MAX, width)
    return lax.all_gather(part, "ep", axis=1, tiled=True)


def line_of(rows):
    for bit in bits_of("dp")[2:]:
        rows = jnp.concatenate([rows, flip(rows, "dp", bit)], axis=0)
    return rows


def all_sets(pieces):
    sets = [pieces]
    for bit in bits_of("ep"):
        sets = sets + [tuple(flip(piece, "ep", bit) for piece in one) for one in sets]
    return sets


def plus(*terms):
    return sum(term.astype(jnp.float32) for term in terms)


def narrow(x):
    return x.astype(jnp.bfloat16)


def scatter_sums(near, far):
    bits = bits_of("ep")[::-1]
    for bit in bits:
        came = flip(far, "ep", bit)
        if bit != bits[-1]:
            both = narrow(plus(near, came))
            near, far = jnp.split(both, 2, axis=0)
    inner_x, inner_y, *outer = bits_of("dp")
    width = near.shape[1]
    half = width // 2
    near = jnp.split(near, 4, axis=0)
    came = jnp.split(came, 4, axis=0)
    diagonal = narrow(plus(near[3], came[3]))
    low = flip(diagonal[:, :half], "dp", inner_x)
    high = flip(diagonal[:, half:], "dp", inner_y)
    to_x = plus(near[1], came[1])
    to_y = plus(near[2], came[2])
    to_x = narrow(jnp.concatenate([to_x[:, :half], to_x[:, half:] + plus(high)], axis=1))
    to_y = narrow(jnp.concatenate([to_y[:, :half] + plus(low), to_y[:, half:]], axis=1))
    from_x = flip(to_x, "dp", inner_x)
    from_y = flip(to_y, "dp", inner_y)
    total = plus(near[0], came[0], from_x, from_y)
    for bit in outer[::-1]:
        mine, other = jnp.split(total, 2, axis=0)
        total = mine + plus(flip(narrow(other), "dp", bit))
    return total


def head_sums(part):
    if lax.axis_size("ep") != 2:
        return lax.psum_scatter(part, "ep", scatter_dimension=0, tiled=True)
    rows = part.shape[0] // 2
    own = lax.axis_index("ep")
    mine = lax.dynamic_slice_in_dim(part, own * rows, rows)
    other = lax.dynamic_slice_in_dim(part, (1 - own) * rows, rows)
    return mine + flip(other, "ep", 1)


def three_terms(x):
    terms = []
    for _ in range(3):
        term = lax.reduce_precision(x, 8, 7)
        terms.append(narrow(term))
        x = x - term
    return terms


def per_device(
    residual,
    queries,
    latent_cache,
    lengths,
    destination,
    w_uv,
    w_o,
    norm_gain,
    experts,
    gate_weights,
    w_gate,
    w_up,
    w_down,
):
    replica_rows = latent_cache.shape[0]
    replicas = destination.shape[0] // replica_rows
    own_replica = lax.axis_index("dp")
    to_box, picker = moves(destination, replica_rows)
    packing = lax.dynamic_slice(
        to_box, (own_replica * MOVE_MAX, own_replica * replica_rows), (MOVE_MAX, replica_rows)
    )
    arrivals = migrate(packing, picker, latent_cache)
    own_leave = jnp.sum(packing.astype(jnp.float32), axis=0) > 0
    fetched = lax.dot_general(
        packing, arrivals, (((0,), (0,)), ((), ())), preferred_element_type=jnp.float32
    ).astype(jnp.bfloat16)
    present = jnp.where(own_leave[:, None], fetched, latent_cache)
    heads_dev = w_uv.shape[0]
    latents = present.reshape(replica_rows, CTX, KV)
    query_rows = queries.reshape(replica_rows, heads_dev, KV)
    scores = (
        jnp.einsum("rhk,rtk->rht", query_rows, latents, preferred_element_type=jnp.float32)
        * score_scale
    )
    in_range = jnp.arange(CTX, dtype=jnp.int32)[None, None, :] < lengths[:, None, None]
    scores = jnp.where(in_range, scores, -jnp.inf)
    row_max = jnp.max(scores, axis=2, keepdims=True)
    weights = jnp.where(in_range, jnp.exp(scores - row_max), 0.0)
    prob_rows = (weights / jnp.sum(weights, axis=2, keepdims=True)).astype(jnp.bfloat16)
    context = narrow(
        jnp.einsum("rht,rtl->rhl", prob_rows, latents[:, :, :LAT], preferred_element_type=jnp.float32)
    )
    width = residual.shape[1]
    half, size = width // 2, width // CHUNKS
    tokens = residual.astype(jnp.float32)

    part, values = values_and_first(jnp.transpose(context, (1, 0, 2)), w_uv, w_o, half)
    hidden_a = tokens[:, :half] + head_sums(part)
    rows_a = narrow(hidden_a * norm_gain[None, :half])
    values, rows_a = lax.optimization_barrier((values, rows_a))
    inner_x, inner_y, *outer = bits_of("dp")
    parts_b = [more_columns(values, w_o, half, size)]
    came = flip(rows_a, "dp", outer[0])
    held_a = jnp.concatenate([rows_a, came], axis=0)
    values, held_a = lax.optimization_barrier((values, held_a))
    parts_b.append(more_columns(values, w_o, half + size, size))
    for bit in outer[1:]:
        held_a = jnp.concatenate([held_a, flip(held_a, "dp", bit)], axis=0)
    x_a = flip(held_a, "dp", inner_x)
    y_a = flip(held_a, "dp", inner_y)

    hidden_b = tokens[:, half:] + head_sums(jnp.concatenate(parts_b, axis=1))
    squares = jnp.sum(hidden_a * hidden_a, axis=1, keepdims=True) + jnp.sum(
        hidden_b * hidden_b, axis=1, keepdims=True
    )
    factor = lax.rsqrt(squares / width + norm_eps)
    expert_ids = jnp.arange(replicas, dtype=jnp.int32)
    matches = experts[:, :, None] == expert_ids[None, None, :]
    gate_sum = jnp.sum(jnp.where(matches, gate_weights[:, :, None], 0.0), axis=1)
    terms = three_terms(gate_sum) + three_terms(factor)
    terms.append(jnp.zeros((tokens.shape[0], GATE_COLS - 3 * replicas - 3), jnp.bfloat16))
    rows_b = jnp.concatenate([narrow(hidden_b * norm_gain[None, half:])] + terms, axis=1)
    held_b = line_of(rows_b)
    d_a = flip(y_a, "dp", inner_x)
    sums = experts_first(all_sets((held_a, x_a, y_a, d_a)), w_gate, w_up)
    x_b = flip(held_b, "dp", inner_x)
    y_b = flip(held_b, "dp", inner_y)
    low_b = flip(y_b[:, :size], "dp", inner_x)
    high_b = flip(x_b[:, size:], "dp", inner_y)
    columns = jnp.arange(GATE_COLS, dtype=jnp.int32)
    gate_mask = (columns < 3 * replicas) & (columns % replicas == own_replica)
    factor_mask = (columns >= 3 * replicas) & (columns < 3 * replicas + 3)
    mask = jnp.stack([gate_mask, factor_mask]).astype(jnp.float32)
    sets_b = all_sets((held_b, x_b, y_b, low_b, high_b))
    far, kept = experts_far(sets_b, mask, sums, w_gate, w_up, w_down)
    mixture = scatter_sums(experts_near(kept, w_down), far)
    hidden = jnp.concatenate([hidden_a, hidden_b], axis=1)
    layer_out = (hidden + mixture).astype(jnp.bfloat16)
    return (layer_out, arrivals)


def solution(mesh):
    in_specs = (
        P(("dp", "ep"), None),
        P("dp", "ep"),
        P("dp", None),
        P("dp"),
        P(),
        P("ep", None, None),
        P("ep", None),
        P(),
        P(("dp", "ep"), None),
        P(("dp", "ep"), None),
        P("dp", None, "ep"),
        P("dp", None, "ep"),
        P("dp", "ep", None),
    )
    out_specs = (P(("dp", "ep"), None), P("dp", None))
    return jax.shard_map(
        per_device, mesh=mesh, in_specs=in_specs, out_specs=out_specs, check_vma=False
    )
```

```python
import functools

import jax
import jax.numpy as jnp
from jax import lax
from jax.experimental import pallas as pl
from jax.experimental.pallas import tpu as pltpu
from jax.sharding import PartitionSpec as P

LAT = 512
KV = 576
V_DIM = 128
MOVE_MAX = 4
CTX = 64
GATE_COLS = 128


score_scale = 192.0 ** (-0.5)
norm_eps = 1e-06


def flip(x, axis, bit):
    pairs = [(i, i ^ bit) for i in range(lax.axis_size(axis))]
    return lax.ppermute(x, axis, pairs)


def bits_of(axis):
    size = lax.axis_size(axis)
    return [1 << b for b in range(size.bit_length() - 1)]


CHUNKS = 4
AHEAD = 3


def vmem_spec():
    return pl.BlockSpec(memory_space=pltpu.VMEM)


def hbm_spec():
    return pl.BlockSpec(memory_space=pltpu.HBM)


def span(n, size):
    return pl.ds(pl.multiple_of(n * size, size), size)


def values_kernel(context, w_uv, w_o, part, values, uv_buf, o_buf, uv_sems, o_sems):
    heads, _, dim = w_uv.shape
    groups = uv_sems.shape[0]
    step = heads // groups
    chunks, depth, width = o_buf.shape

    def copy_uv(g):
        own = pl.ds(g * step, step)
        return pltpu.make_async_copy(w_uv.at[own], uv_buf.at[own], uv_sems.at[g])

    def copy_o(n):
        rows = pl.ds(n * depth, depth)
        return pltpu.make_async_copy(w_o.at[rows, pl.ds(0, width)], o_buf.at[n], o_sems.at[n])

    for g in range(groups):
        copy_uv(g).start()
    for n in range(AHEAD):
        copy_o(n).start()
    for g in range(groups):
        copy_uv(g).wait()
        for h in range(g * step, (g + 1) * step):
            values[:, h * dim : (h + 1) * dim] = jnp.dot(
                context[h], uv_buf[h], preferred_element_type=jnp.float32
            ).astype(jnp.bfloat16)
    for n in range(chunks):
        copy_o(n).wait()
        if n + AHEAD < chunks:
            copy_o(n + AHEAD).start()
        product = jnp.dot(
            values[:, n * depth : (n + 1) * depth], o_buf[n], preferred_element_type=jnp.float32
        )
        if n == 0:
            part[...] = product
        else:
            part[...] += product


def values_and_first(context, w_uv, w_o, width):
    heads, rows, latent = context.shape
    depth = w_o.shape[0]
    chunks = 8
    groups = 4 if heads % 4 == 0 else 1
    return pl.pallas_call(
        values_kernel,
        out_shape=(
            jax.ShapeDtypeStruct((rows, width), jnp.float32),
            jax.ShapeDtypeStruct((rows, depth), jnp.bfloat16),
        ),
        in_specs=[vmem_spec(), hbm_spec(), hbm_spec()],
        out_specs=(vmem_spec(), vmem_spec()),
        scratch_shapes=[
            pltpu.VMEM(w_uv.shape, jnp.bfloat16),
            pltpu.VMEM((chunks, depth // chunks, width), jnp.bfloat16),
            pltpu.SemaphoreType.DMA((groups,)),
            pltpu.SemaphoreType.DMA((chunks,)),
        ],
        compiler_params=pltpu.CompilerParams(vmem_limit_bytes=44 << 20),
        cost_estimate=pl.CostEstimate(
            flops=2 * rows * depth * (width + latent),
            bytes_accessed=2 * depth * (width + latent),
            transcendentals=0,
        ),
        name="values_and_first",
    )(context, w_uv, w_o)


def columns_kernel(start, values, w_o, part, o_buf, o_sems):
    chunks, depth, width = o_buf.shape

    def copy_o(n):
        rows = pl.ds(n * depth, depth)
        return pltpu.make_async_copy(w_o.at[rows, pl.ds(start, width)], o_buf.at[n], o_sems.at[n])

    for n in range(AHEAD):
        copy_o(n).start()
    for n in range(chunks):
        copy_o(n).wait()
        if n + AHEAD < chunks:
            copy_o(n + AHEAD).start()
        product = jnp.dot(
            values[:, n * depth : (n + 1) * depth], o_buf[n], preferred_element_type=jnp.float32
        )
        if n == 0:
            part[...] = product
        else:
            part[...] += product


def more_columns(values, w_o, start, width):
    rows, depth = values.shape
    chunks = 8
    return pl.pallas_call(
        functools.partial(columns_kernel, start),
        out_shape=jax.ShapeDtypeStruct((rows, width), jnp.float32),
        in_specs=[vmem_spec(), hbm_spec()],
        out_specs=vmem_spec(),
        scratch_shapes=[
            pltpu.VMEM((chunks, depth // chunks, width), jnp.bfloat16),
            pltpu.SemaphoreType.DMA((chunks,)),
        ],
        compiler_params=pltpu.CompilerParams(vmem_limit_bytes=24 << 20),
        cost_estimate=pl.CostEstimate(
            flops=2 * rows * depth * width, bytes_accessed=2 * depth * width, transcendentals=0
        ),
        name="more_columns",
    )(values, w_o)


def first_kernel(set_count, *refs):
    flat, refs = refs[: 5 * set_count], refs[5 * set_count :]
    sets = [flat[5 * n : 5 * n + 5] for n in range(set_count)]
    w_gate, w_up, gate_acc, up_acc, gate_buf, up_buf, sems = refs
    chunks, size, _ = gate_buf.shape

    def copies_in(n):
        return (
            pltpu.make_async_copy(w_gate.at[0, span(n, size)], gate_buf.at[n], sems.at[0, n]),
            pltpu.make_async_copy(w_up.at[0, span(n, size)], up_buf.at[n], sems.at[1, n]),
        )

    for n in range(chunks):
        for copy in copies_in(n):
            copy.start()
    for n in range(chunks):
        parts = []
        for own, near_x, near_y, low, high in sets:
            parts += [ref[:, n * size : (n + 1) * size] for ref in (own, near_x, near_y)]
            parts.append((low, high)[n][...])
        rows = jnp.concatenate(parts, axis=0)
        for copy in copies_in(n):
            copy.wait()
        gate_part = jnp.dot(rows, gate_buf[n], preferred_element_type=jnp.float32)
        up_part = jnp.dot(rows, up_buf[n], preferred_element_type=jnp.float32)
        if n == 0:
            gate_acc[...] = gate_part
            up_acc[...] = up_part
        else:
            gate_acc[...] += gate_part
            up_acc[...] += up_part


def experts_first(sets, w_gate, w_up):
    width, hidden_units = w_gate.shape[1:]
    size = width // CHUNKS
    flat = [piece for pieces in sets for piece in pieces]
    rows = sum(piece.shape[0] for pieces in sets for piece in pieces[:4])
    sums = jax.ShapeDtypeStruct((rows, hidden_units), jnp.float32)
    return pl.pallas_call(
        functools.partial(first_kernel, len(sets)),
        out_shape=(sums, sums),
        in_specs=[vmem_spec()] * len(flat) + [hbm_spec()] * 2,
        out_specs=(vmem_spec(), vmem_spec()),
        scratch_shapes=[
            pltpu.VMEM((CHUNKS // 2, size, hidden_units), jnp.bfloat16),
            pltpu.VMEM((CHUNKS // 2, size, hidden_units), jnp.bfloat16),
            pltpu.SemaphoreType.DMA((2, CHUNKS // 2)),
        ],
        compiler_params=pltpu.CompilerParams(vmem_limit_bytes=32 << 20),
        cost_estimate=pl.CostEstimate(
            flops=2 * rows * width * hidden_units,
            bytes_accessed=2 * width * hidden_units + rows * width,
            transcendentals=0,
        ),
        name="experts_first",
    )(*flat, w_gate, w_up)


def far_kernel(set_count, *refs):
    flat, refs = refs[: 5 * set_count], refs[5 * set_count :]
    sets = [flat[5 * n : 5 * n + 5] for n in range(set_count)]
    mask, gate_first, up_first, w_gate, w_up, w_down, far, kept = refs[:8]
    gate_buf, up_buf, down_buf, gate_acc, up_acc, act, sems = refs[8:]
    chunks, size, _ = gate_buf.shape
    half = w_gate.shape[1] // 2
    half_rows = far.shape[0]

    def copies_in(n):
        rows = pl.ds(half + n * size, size)
        return (
            pltpu.make_async_copy(w_gate.at[0, rows], gate_buf.at[n], sems.at[0, n]),
            pltpu.make_async_copy(w_up.at[0, rows], up_buf.at[n], sems.at[1, n]),
        )

    def copy_down(n):
        return pltpu.make_async_copy(w_down.at[0, :, span(n, size)], down_buf.at[n], sems.at[2, n])

    for n in range(chunks):
        for copy in copies_in(n):
            copy.start()
    for n in range(CHUNKS):
        copy_down(n).start()
    tails = []
    for own, near_x, near_y, low, high in sets:
        tails += [ref[:, half:] for ref in (own, near_x, near_y)] + [high[:, size:]]
    terms = jnp.concatenate(tails, axis=0).astype(jnp.float32)
    gates = jnp.sum(terms * mask[0:1], axis=1, keepdims=True)
    factors = jnp.sum(terms * mask[1:2], axis=1, keepdims=True)
    for n in range(chunks):
        parts = []
        for own, near_x, near_y, low, high in sets:
            parts += [ref[:, n * size : (n + 1) * size] for ref in (own, near_x, near_y)]
            parts.append((low, high)[n][:, :size])
        rows = jnp.concatenate(parts, axis=0)
        for copy in copies_in(n):
            copy.wait()
        before = (gate_first, up_first) if n == 0 else (gate_acc, up_acc)
        gate_acc[...] = before[0][...] + jnp.dot(
            rows, gate_buf[n], preferred_element_type=jnp.float32
        )
        up_acc[...] = before[1][...] + jnp.dot(rows, up_buf[n], preferred_element_type=jnp.float32)
    gated = gate_acc[...] * factors
    raised = up_acc[...] * factors
    act[...] = (gated / (1.0 + jnp.exp(-gated)) * raised * gates).astype(jnp.bfloat16)
    kept[...] = act[:half_rows]

    @pl.loop(0, CHUNKS)
    def _(n):
        copy_down(n).wait()
        far[:, span(n, size)] = jnp.dot(
            act[half_rows:], down_buf[n], preferred_element_type=jnp.float32
        ).astype(jnp.bfloat16)


def experts_far(sets, mask, sums, w_gate, w_up, w_down):
    width, hidden_units = w_gate.shape[1:]
    rows = sums[0].shape[0]
    size = width // CHUNKS
    flat = [piece for pieces in sets for piece in pieces]
    return pl.pallas_call(
        functools.partial(far_kernel, len(sets)),
        out_shape=(
            jax.ShapeDtypeStruct((rows // 2, width), jnp.bfloat16),
            jax.ShapeDtypeStruct((rows // 2, hidden_units), jnp.bfloat16),
        ),
        in_specs=[vmem_spec()] * (len(flat) + 3) + [hbm_spec()] * 3,
        out_specs=(vmem_spec(), vmem_spec()),
        scratch_shapes=[
            pltpu.VMEM((CHUNKS // 2, size, hidden_units), jnp.bfloat16),
            pltpu.VMEM((CHUNKS // 2, size, hidden_units), jnp.bfloat16),
            pltpu.VMEM((CHUNKS, hidden_units, size), jnp.bfloat16),
            pltpu.VMEM((rows, hidden_units), jnp.float32),
            pltpu.VMEM((rows, hidden_units), jnp.float32),
            pltpu.VMEM((rows, hidden_units), jnp.bfloat16),
            pltpu.SemaphoreType.DMA((3, CHUNKS)),
        ],
        compiler_params=pltpu.CompilerParams(vmem_limit_bytes=48 << 20),
        cost_estimate=pl.CostEstimate(
            flops=3 * rows * width * hidden_units,
            bytes_accessed=4 * width * hidden_units + 3 * rows * width,
            transcendentals=rows * hidden_units,
        ),
        name="experts_far",
    )(*flat, mask, *sums, w_gate, w_up, w_down)


def down_kernel(kept, w_down, near, down_buf, sems):
    size = down_buf.shape[2]

    def copy(n):
        columns = pl.ds(pl.multiple_of(n * size, size), size)
        return pltpu.make_async_copy(w_down.at[0, :, columns], down_buf.at[n], sems.at[n])

    for n in range(CHUNKS):
        copy(n).start()

    @pl.loop(0, CHUNKS)
    def _(n):
        copy(n).wait()
        columns = pl.ds(pl.multiple_of(n * size, size), size)
        near[:, columns] = jnp.dot(
            kept[...], down_buf[n], preferred_element_type=jnp.float32
        ).astype(jnp.bfloat16)


def experts_near(kept, w_down):
    rows, hidden_units = kept.shape
    width = w_down.shape[2]
    size = width // CHUNKS
    return pl.pallas_call(
        down_kernel,
        out_shape=jax.ShapeDtypeStruct((rows, width), jnp.bfloat16),
        in_specs=[vmem_spec(), hbm_spec()],
        out_specs=vmem_spec(),
        scratch_shapes=[
            pltpu.VMEM((CHUNKS, hidden_units, size), jnp.bfloat16),
            pltpu.SemaphoreType.DMA((CHUNKS,)),
        ],
        compiler_params=pltpu.CompilerParams(vmem_limit_bytes=32 << 20),
        cost_estimate=pl.CostEstimate(
            flops=2 * rows * width * hidden_units,
            bytes_accessed=2 * width * hidden_units + 2 * rows * width,
            transcendentals=0,
        ),
        name="experts_near",
    )(kept, w_down)


def moves(destination, replica_rows):
    slots = destination.shape[0]
    replicas = slots // replica_rows
    ids = jnp.arange(slots, dtype=jnp.int32)
    home = ids // replica_rows
    leaving = destination // replica_rows != home
    earlier = (home[:, None] == home[None, :]) & (ids[:, None] < ids[None, :])
    rank = jnp.sum(jnp.where(earlier & leaving[:, None], 1, 0), axis=0)
    box = jnp.where(leaving, home * MOVE_MAX + rank, -1)
    boxes = jnp.arange(replicas * MOVE_MAX, dtype=jnp.int32)
    to_box = (boxes[:, None] == box[None, :]).astype(jnp.bfloat16)
    lands = (ids[:, None] == destination[None, :]).astype(jnp.bfloat16)
    target = jnp.dot(to_box, lands, preferred_element_type=jnp.float32).astype(jnp.bfloat16)
    picker = lax.dot_general(
        target, to_box, (((1,), (1,)), ((), ())), preferred_element_type=jnp.float32
    ).astype(jnp.bfloat16)
    return to_box, picker


def migrate(packing, picker, latent_cache):
    replicas = lax.axis_size("dp")
    ep_count = lax.axis_size("ep")
    width = latent_cache.shape[1] // ep_count
    share = width // replicas
    own = lax.dynamic_slice_in_dim(latent_cache, lax.axis_index("ep") * width, width, axis=1)
    outbox = jnp.dot(packing, own, preferred_element_type=jnp.float32).astype(jnp.bfloat16)
    outbox = outbox.reshape(MOVE_MAX, replicas, share).transpose(1, 0, 2)
    met = lax.all_to_all(outbox, "dp", split_axis=0, concat_axis=0)
    sorted_rows = jnp.dot(
        picker, met.reshape(replicas * MOVE_MAX, share), preferred_element_type=jnp.float32
    ).astype(jnp.bfloat16)
    taken = lax.all_to_all(
        sorted_rows.reshape(replicas, MOVE_MAX, share), "dp", split_axis=0, concat_axis=0
    )
    part = taken.transpose(1, 0, 2).reshape(MOVE_MAX, width)
    return lax.all_gather(part, "ep", axis=1, tiled=True)


def all_sets(pieces):
    sets = [pieces]
    for bit in bits_of("ep"):
        sets = sets + [tuple(flip(piece, "ep", bit) for piece in one) for one in sets]
    return sets


def dp_bits():
    inner_x, inner_y, *outer = bits_of("dp")
    return inner_x, inner_y, outer[::-1]


def plus(*terms):
    return sum(term.astype(jnp.float32) for term in terms)


def narrow(x):
    return x.astype(jnp.bfloat16)


def scatter_sums(near, far):
    bits = bits_of("ep")[::-1]
    for bit in bits:
        came = flip(far, "ep", bit)
        if bit != bits[-1]:
            both = narrow(plus(near, came))
            near, far = jnp.split(both, 2, axis=0)
    inner_x, inner_y, outer = dp_bits()
    width = near.shape[1]
    half = width // 2
    near = jnp.split(near, 4, axis=0)
    came = jnp.split(came, 4, axis=0)
    diagonal = narrow(plus(near[3], came[3]))
    low = flip(diagonal[:, :half], "dp", inner_x)
    high = flip(diagonal[:, half:], "dp", inner_y)
    to_x = plus(near[1], came[1])
    to_y = plus(near[2], came[2])
    to_x = narrow(jnp.concatenate([to_x[:, :half], to_x[:, half:] + plus(high)], axis=1))
    to_y = narrow(jnp.concatenate([to_y[:, :half] + plus(low), to_y[:, half:]], axis=1))
    from_x = flip(to_x, "dp", inner_x)
    from_y = flip(to_y, "dp", inner_y)
    total = plus(near[0], came[0], from_x, from_y)
    for bit in outer[::-1]:
        mine, other = jnp.split(total, 2, axis=0)
        total = mine + plus(flip(narrow(other), "dp", bit))
    return total


def head_sums(part):
    if lax.axis_size("ep") != 2:
        return lax.psum_scatter(part, "ep", scatter_dimension=0, tiled=True)
    rows = part.shape[0] // 2
    own = lax.axis_index("ep")
    mine = lax.dynamic_slice_in_dim(part, own * rows, rows)
    other = lax.dynamic_slice_in_dim(part, (1 - own) * rows, rows)
    return mine + flip(other, "ep", 1)


def three_terms(x):
    terms = []
    for _ in range(3):
        term = lax.reduce_precision(x, 8, 7)
        terms.append(narrow(term))
        x = x - term
    return terms


def per_device(
    residual,
    queries,
    latent_cache,
    lengths,
    destination,
    w_uv,
    w_o,
    norm_gain,
    experts,
    gate_weights,
    w_gate,
    w_up,
    w_down,
):
    w_uv, w_o, w_gate, w_up, w_down = (
        pltpu.with_memory_space_constraint(w, pltpu.HBM) for w in (w_uv, w_o, w_gate, w_up, w_down)
    )
    replica_rows = latent_cache.shape[0]
    replicas = destination.shape[0] // replica_rows
    own_replica = lax.axis_index("dp")
    to_box, picker = moves(destination, replica_rows)
    packing = lax.dynamic_slice(
        to_box, (own_replica * MOVE_MAX, own_replica * replica_rows), (MOVE_MAX, replica_rows)
    )
    arrivals = migrate(packing, picker, latent_cache)
    own_leave = jnp.sum(packing.astype(jnp.float32), axis=0) > 0
    fetched = lax.dot_general(
        packing, arrivals, (((0,), (0,)), ((), ())), preferred_element_type=jnp.float32
    ).astype(jnp.bfloat16)
    present = jnp.where(own_leave[:, None], fetched, latent_cache)
    heads_dev = w_uv.shape[0]
    latents = present.reshape(replica_rows, CTX, KV)
    query_rows = queries.reshape(replica_rows, heads_dev, KV)
    scores = (
        jnp.einsum("rhk,rtk->rht", query_rows, latents, preferred_element_type=jnp.float32)
        * score_scale
    )
    in_range = jnp.arange(CTX, dtype=jnp.int32)[None, None, :] < lengths[:, None, None]
    scores = jnp.where(in_range, scores, -jnp.inf)
    row_max = jnp.max(scores, axis=2, keepdims=True)
    weights = jnp.where(in_range, jnp.exp(scores - row_max), 0.0)
    prob_rows = (weights / jnp.sum(weights, axis=2, keepdims=True)).astype(jnp.bfloat16)
    context = narrow(
        jnp.einsum("rht,rtl->rhl", prob_rows, latents[:, :, :LAT], preferred_element_type=jnp.float32)
    )
    width = residual.shape[1]
    half, size = width // 2, width // CHUNKS
    tokens = residual.astype(jnp.float32)

    part, values = values_and_first(jnp.transpose(context, (1, 0, 2)), w_uv, w_o, half)
    hidden_a = tokens[:, :half] + head_sums(part)
    rows_a = narrow(hidden_a * norm_gain[None, :half])
    values, rows_a = lax.optimization_barrier((values, rows_a))
    inner_x, inner_y, outer = dp_bits()
    early = half * 2 // 5 // 128 * 128
    parts_b = [more_columns(values, w_o, half, early)]
    came, parts_b = lax.optimization_barrier((flip(rows_a, "dp", outer[0]), parts_b))
    held_a = jnp.concatenate([rows_a, came], axis=0)
    values, held_a = lax.optimization_barrier((values, held_a))
    parts_b.append(more_columns(values, w_o, half + early, half - early))
    for bit in outer[1:]:
        held_a = jnp.concatenate([held_a, flip(held_a, "dp", bit)], axis=0)
    parts_b, held_a = lax.optimization_barrier((parts_b, held_a))
    x_a = flip(held_a, "dp", inner_x)
    y_a = flip(held_a, "dp", inner_y)

    hidden_b = tokens[:, half:] + head_sums(jnp.concatenate(parts_b, axis=1))
    squares = jnp.sum(hidden_a * hidden_a, axis=1, keepdims=True) + jnp.sum(
        hidden_b * hidden_b, axis=1, keepdims=True
    )
    factor = lax.rsqrt(squares / width + norm_eps)
    expert_ids = jnp.arange(replicas, dtype=jnp.int32)
    matches = experts[:, :, None] == expert_ids[None, None, :]
    gate_sum = jnp.sum(jnp.where(matches, gate_weights[:, :, None], 0.0), axis=1)
    terms = three_terms(gate_sum) + three_terms(factor)
    terms.append(jnp.zeros((tokens.shape[0], GATE_COLS - 3 * replicas - 3), jnp.bfloat16))
    rows_b = jnp.concatenate([narrow(hidden_b * norm_gain[None, half:])] + terms, axis=1)
    held_b = jnp.concatenate([rows_b, flip(rows_b, "dp", outer[0])], axis=0)
    held_b, x_a, y_a = lax.optimization_barrier((held_b, x_a, y_a))
    low_a = flip(y_a[:, :size], "dp", inner_x)
    high_a = flip(x_a[:, size:], "dp", inner_y)
    for bit in outer[1:]:
        held_b = jnp.concatenate([held_b, flip(held_b, "dp", bit)], axis=0)
    held_b, low_a, high_a = lax.optimization_barrier((held_b, low_a, high_a))
    x_b = flip(held_b, "dp", inner_x)
    y_b = flip(held_b, "dp", inner_y)
    sums = experts_first(all_sets((held_a, x_a, y_a, low_a, high_a)), w_gate, w_up)
    low_b = flip(y_b[:, :size], "dp", inner_x)
    high_b = flip(x_b[:, size:], "dp", inner_y)
    low_b, high_b, sums = lax.optimization_barrier((low_b, high_b, sums))
    columns = jnp.arange(GATE_COLS, dtype=jnp.int32)
    gate_mask = (columns < 3 * replicas) & (columns % replicas == own_replica)
    factor_mask = (columns >= 3 * replicas) & (columns < 3 * replicas + 3)
    mask = jnp.stack([gate_mask, factor_mask]).astype(jnp.float32)
    sets_b = all_sets((held_b, x_b, y_b, low_b, high_b))
    far, kept = experts_far(sets_b, mask, sums, w_gate, w_up, w_down)
    mixture = scatter_sums(experts_near(kept, w_down), far)
    hidden = jnp.concatenate([hidden_a, hidden_b], axis=1)
    layer_out = (hidden + mixture).astype(jnp.bfloat16)
    return (layer_out, arrivals)


def solution(mesh):
    in_specs = (
        P(("dp", "ep"), None),
        P("dp", "ep"),
        P("dp", None),
        P("dp"),
        P(),
        P("ep", None, None),
        P("ep", None),
        P(),
        P(("dp", "ep"), None),
        P(("dp", "ep"), None),
        P("dp", None, "ep"),
        P("dp", None, "ep"),
        P("dp", "ep", None),
    )
    out_specs = (P(("dp", "ep"), None), P("dp", None))
    return jax.shard_map(
        per_device, mesh=mesh, in_specs=in_specs, out_specs=out_specs, check_vma=False
    )
```

```python
import functools

import jax
import jax.numpy as jnp
from jax import lax
from jax.experimental import pallas as pl
from jax.experimental.pallas import tpu as pltpu
from jax.sharding import PartitionSpec as P

LAT = 512
KV = 576
V_DIM = 128
MOVE_MAX = 4
CTX = 64
GATE_COLS = 128


score_scale = 192.0 ** (-0.5)
norm_eps = 1e-06


def flip(x, axis, bit):
    pairs = [(i, i ^ bit) for i in range(lax.axis_size(axis))]
    return lax.ppermute(x, axis, pairs)


def bits_of(axis):
    size = lax.axis_size(axis)
    return [1 << b for b in range(size.bit_length() - 1)]


CHUNKS = 4
IN_FLIGHT = 10 << 20


def vmem_spec():
    return pl.BlockSpec(memory_space=pltpu.VMEM)


def hbm_spec():
    return pl.BlockSpec(memory_space=pltpu.HBM)


def span(n, size):
    return pl.ds(pl.multiple_of(n * size, size), size)


def attention_kernel(
    moved, lengths, queries, cached, arrived, w_uv, w_o, part, values,
    keys, context, uv_buf, o_buf, uv_sems, o_sems,
):
    requests, heads, _ = queries.shape
    latent, dim = w_uv.shape[1:]
    groups = uv_sems.shape[0]
    step = heads // groups
    chunks, depth, width = o_buf.shape

    def copy_uv(g):
        own = pl.ds(g * step, step)
        return pltpu.make_async_copy(w_uv.at[own], uv_buf.at[own], uv_sems.at[g])

    def copy_o(n):
        rows = pl.ds(n * depth, depth)
        return pltpu.make_async_copy(w_o.at[rows, pl.ds(0, width)], o_buf.at[n], o_sems.at[n])

    for g in range(groups):
        copy_uv(g).start()
    ahead = min(chunks, max(2, 2 * IN_FLIGHT // (2 * depth * width)))
    for n in range(ahead):
        copy_o(n).start()
    for i in range(requests):
        row = moved[i]
        keys[i] = jnp.where(row >= 0, arrived[jnp.maximum(row, 0)], cached[i])
    scores, limits = [], []
    for i in range(requests):
        score = lax.dot_general(
            queries[i], keys[i], (((1,), (1,)), ((), ())), preferred_element_type=jnp.float32
        )
        scores.append(score)
        limits.append(jnp.full(score.shape, lengths[i], jnp.int32))
    scores = jnp.concatenate(scores, axis=0) * score_scale
    in_range = lax.broadcasted_iota(jnp.int32, scores.shape, 1) < jnp.concatenate(limits, axis=0)
    scores = jnp.where(in_range, scores, -jnp.inf)
    row_max = jnp.max(scores, axis=1, keepdims=True)
    weights = jnp.where(in_range, jnp.exp(scores - row_max), 0.0)
    probs = (weights / jnp.sum(weights, axis=1, keepdims=True)).astype(jnp.bfloat16)
    for i in range(requests):
        context[:, i, :] = jnp.dot(
            probs[i * heads : (i + 1) * heads],
            keys[i, :, :latent],
            preferred_element_type=jnp.float32,
        )
    for g in range(groups):
        copy_uv(g).wait()
        for h in range(g * step, (g + 1) * step):
            values[:, h * dim : (h + 1) * dim] = jnp.dot(
                context[h].astype(jnp.bfloat16), uv_buf[h], preferred_element_type=jnp.float32
            ).astype(jnp.bfloat16)
    for n in range(chunks):
        copy_o(n).wait()
        if n + ahead < chunks:
            copy_o(n + ahead).start()
        product = jnp.dot(
            values[:, n * depth : (n + 1) * depth], o_buf[n], preferred_element_type=jnp.float32
        )
        if n == 0:
            part[...] = product
        else:
            part[...] += product


def attention_and_first(moved, lengths, queries, cached, arrived, w_uv, w_o, width):
    requests, heads, key_width = queries.shape
    latent = w_uv.shape[1]
    depth = w_o.shape[0]
    chunks = 8
    groups = 4 if heads % 4 == 0 else 1
    smem = pl.BlockSpec(memory_space=pltpu.SMEM)
    return pl.pallas_call(
        attention_kernel,
        out_shape=(
            jax.ShapeDtypeStruct((requests, width), jnp.float32),
            jax.ShapeDtypeStruct((requests, depth), jnp.bfloat16),
        ),
        in_specs=[smem, smem] + [vmem_spec()] * 3 + [hbm_spec()] * 2,
        out_specs=(vmem_spec(), vmem_spec()),
        scratch_shapes=[
            pltpu.VMEM(cached.shape, jnp.bfloat16),
            pltpu.VMEM((heads, requests, latent), jnp.float32),
            pltpu.VMEM(w_uv.shape, jnp.bfloat16),
            pltpu.VMEM((chunks, depth // chunks, width), jnp.bfloat16),
            pltpu.SemaphoreType.DMA((groups,)),
            pltpu.SemaphoreType.DMA((chunks,)),
        ],
        compiler_params=pltpu.CompilerParams(vmem_limit_bytes=48 << 20),
        cost_estimate=pl.CostEstimate(
            flops=2 * requests * depth * (width + latent),
            bytes_accessed=2 * depth * (width + latent),
            transcendentals=requests * heads * CTX,
        ),
        name="attention_and_first",
    )(moved, lengths, queries, cached, arrived, w_uv, w_o)


def columns_kernel(start, values, w_o, part, o_buf, o_sems):
    chunks, depth, width = o_buf.shape

    def copy_o(n):
        rows = pl.ds(n * depth, depth)
        return pltpu.make_async_copy(w_o.at[rows, pl.ds(start, width)], o_buf.at[n], o_sems.at[n])

    ahead = min(chunks, max(2, IN_FLIGHT // (2 * depth * width)))
    for n in range(ahead):
        copy_o(n).start()
    for n in range(chunks):
        copy_o(n).wait()
        if n + ahead < chunks:
            copy_o(n + ahead).start()
        product = jnp.dot(
            values[:, n * depth : (n + 1) * depth], o_buf[n], preferred_element_type=jnp.float32
        )
        if n == 0:
            part[...] = product
        else:
            part[...] += product


def more_columns(values, w_o, start, width):
    rows, depth = values.shape
    chunks = 8
    return pl.pallas_call(
        functools.partial(columns_kernel, start),
        out_shape=jax.ShapeDtypeStruct((rows, width), jnp.float32),
        in_specs=[vmem_spec(), hbm_spec()],
        out_specs=vmem_spec(),
        scratch_shapes=[
            pltpu.VMEM((chunks, depth // chunks, width), jnp.bfloat16),
            pltpu.SemaphoreType.DMA((chunks,)),
        ],
        compiler_params=pltpu.CompilerParams(vmem_limit_bytes=24 << 20),
        cost_estimate=pl.CostEstimate(
            flops=2 * rows * depth * width, bytes_accessed=2 * depth * width, transcendentals=0
        ),
        name="more_columns",
    )(values, w_o)


def first_kernel(set_count, *refs):
    flat, refs = refs[: 5 * set_count], refs[5 * set_count :]
    sets = [flat[5 * n : 5 * n + 5] for n in range(set_count)]
    w_gate, w_up, gate_acc, up_acc, gate_buf, up_buf, sems = refs
    chunks, size, _ = gate_buf.shape

    def copies_in(n):
        return (
            pltpu.make_async_copy(w_gate.at[0, span(n, size)], gate_buf.at[n], sems.at[0, n]),
            pltpu.make_async_copy(w_up.at[0, span(n, size)], up_buf.at[n], sems.at[1, n]),
        )

    for n in range(chunks):
        for copy in copies_in(n):
            copy.start()
    for n in range(chunks):
        parts = []
        for own, near_x, near_y, low, high in sets:
            parts += [ref[:, n * size : (n + 1) * size] for ref in (own, near_x, near_y)]
            parts.append((low, high)[n][...])
        rows = jnp.concatenate(parts, axis=0)
        for copy in copies_in(n):
            copy.wait()
        gate_part = jnp.dot(rows, gate_buf[n], preferred_element_type=jnp.float32)
        up_part = jnp.dot(rows, up_buf[n], preferred_element_type=jnp.float32)
        if n == 0:
            gate_acc[...] = gate_part
            up_acc[...] = up_part
        else:
            gate_acc[...] += gate_part
            up_acc[...] += up_part


def experts_first(sets, w_gate, w_up):
    width, hidden_units = w_gate.shape[1:]
    size = width // CHUNKS
    flat = [piece for pieces in sets for piece in pieces]
    rows = sum(piece.shape[0] for pieces in sets for piece in pieces[:4])
    sums = jax.ShapeDtypeStruct((rows, hidden_units), jnp.float32)
    return pl.pallas_call(
        functools.partial(first_kernel, len(sets)),
        out_shape=(sums, sums),
        in_specs=[vmem_spec()] * len(flat) + [hbm_spec()] * 2,
        out_specs=(vmem_spec(), vmem_spec()),
        scratch_shapes=[
            pltpu.VMEM((CHUNKS // 2, size, hidden_units), jnp.bfloat16),
            pltpu.VMEM((CHUNKS // 2, size, hidden_units), jnp.bfloat16),
            pltpu.SemaphoreType.DMA((2, CHUNKS // 2)),
        ],
        compiler_params=pltpu.CompilerParams(vmem_limit_bytes=32 << 20),
        cost_estimate=pl.CostEstimate(
            flops=2 * rows * width * hidden_units,
            bytes_accessed=2 * width * hidden_units + rows * width,
            transcendentals=0,
        ),
        name="experts_first",
    )(*flat, w_gate, w_up)


def hold_kernel(after, w_gate, w_up, w_down, gate, up, down, done, sems):
    half = gate.shape[0]
    parts = sems.shape[1]

    def copies(n):
        size = half // parts
        rows = pl.ds(n * size, size)
        later = pl.ds(half + n * size, size)
        units = pl.ds(n * (down.shape[0] // parts), down.shape[0] // parts)
        return (
            pltpu.make_async_copy(w_gate.at[0, later], gate.at[rows], sems.at[0, n]),
            pltpu.make_async_copy(w_up.at[0, later], up.at[rows], sems.at[1, n]),
            pltpu.make_async_copy(w_down.at[0, units], down.at[units], sems.at[2, n]),
        )

    for n in range(parts):
        for copy in copies(n):
            copy.start()
    done[...] = after[...]
    for n in range(parts):
        for copy in copies(n):
            copy.wait()


def hold_weights(after, w_gate, w_up, w_down):
    width, hidden_units = w_gate.shape[1:]
    half = width // 2
    return pl.pallas_call(
        hold_kernel,
        out_shape=(
            pltpu.VMEM((half, hidden_units), jnp.bfloat16),
            pltpu.VMEM((half, hidden_units), jnp.bfloat16),
            pltpu.VMEM((hidden_units, width), jnp.bfloat16),
            jax.ShapeDtypeStruct(after.shape, after.dtype),
        ),
        in_specs=[vmem_spec()] + [hbm_spec()] * 3,
        out_specs=(vmem_spec(),) * 4,
        scratch_shapes=[pltpu.SemaphoreType.DMA((3, 2))],
        compiler_params=pltpu.CompilerParams(vmem_limit_bytes=4 << 20),
        cost_estimate=pl.CostEstimate(
            flops=0, bytes_accessed=4 * width * hidden_units, transcendentals=0
        ),
        name="hold_weights",
    )(after, w_gate, w_up, w_down)


def held(array):
    return pltpu.with_memory_space_constraint(array, pltpu.VMEM)


def second_kernel(set_count, *refs):
    flat, refs = refs[: 5 * set_count], refs[5 * set_count :]
    sets = [flat[5 * n : 5 * n + 5] for n in range(set_count)]
    mask, gate_first, up_first, w_gate, w_up, w_down = refs[:6]
    near, far, rest, gate_acc, up_acc, act = refs[6:]
    half = w_gate.shape[0]
    size = half // 2
    line = near.shape[0] * 2 // set_count
    tails = []
    for own, near_x, near_y, low, high in sets:
        tails += [ref[:, half:] for ref in (own, near_x, near_y)] + [high[:, size:]]
    terms = jnp.concatenate(tails, axis=0).astype(jnp.float32)
    gates = jnp.sum(terms * mask[0:1], axis=1, keepdims=True)
    factors = jnp.sum(terms * mask[1:2], axis=1, keepdims=True)
    for n in range(2):
        parts = []
        for own, near_x, near_y, low, high in sets:
            parts += [ref[:, n * size : (n + 1) * size] for ref in (own, near_x, near_y)]
            parts.append((low, high)[n][:, :size])
        rows = jnp.concatenate(parts, axis=0)
        before = (gate_first, up_first) if n == 0 else (gate_acc, up_acc)
        depth = slice(n * size, (n + 1) * size)
        gate_acc[...] = before[0][...] + jnp.dot(
            rows, w_gate[depth], preferred_element_type=jnp.float32
        )
        up_acc[...] = before[1][...] + jnp.dot(
            rows, w_up[depth], preferred_element_type=jnp.float32
        )
    gated = gate_acc[...] * factors
    raised = up_acc[...] * factors
    act[...] = (gated / (1.0 + jnp.exp(-gated)) * raised * gates).astype(jnp.bfloat16)
    corners = []
    for n in range(set_count):
        rest[n * 3 * line : (n + 1) * 3 * line] = act[n * 4 * line : (n * 4 + 3) * line]
        corners.append(act[(n * 4 + 3) * line : (n + 1) * 4 * line])
    corner = jnp.concatenate(corners, axis=0)
    mine = near.shape[0]

    @pl.loop(0, CHUNKS)
    def _(n):
        columns = span(n, size)
        product = jnp.dot(corner, w_down[:, columns], preferred_element_type=jnp.float32)
        near[:, columns] = product[:mine].astype(jnp.bfloat16)
        far[:, columns] = product[mine:].astype(jnp.bfloat16)


def experts_second(sets, mask, sums, w_gate, w_up, w_down):
    hidden_units, width = w_down.shape
    rows = sums[0].shape[0]
    flat = [piece for pieces in sets for piece in pieces]
    corner = jax.ShapeDtypeStruct((rows // 8, width), jnp.bfloat16)
    return pl.pallas_call(
        functools.partial(second_kernel, len(sets)),
        out_shape=(
            corner,
            corner,
            jax.ShapeDtypeStruct((rows // 4 * 3, hidden_units), jnp.bfloat16),
        ),
        in_specs=[vmem_spec()] * (len(flat) + 6),
        out_specs=(vmem_spec(),) * 3,
        scratch_shapes=[
            pltpu.VMEM((rows, hidden_units), jnp.float32),
            pltpu.VMEM((rows, hidden_units), jnp.float32),
            pltpu.VMEM((rows, hidden_units), jnp.bfloat16),
        ],
        compiler_params=pltpu.CompilerParams(vmem_limit_bytes=24 << 20),
        cost_estimate=pl.CostEstimate(
            flops=3 * rows * width * hidden_units,
            bytes_accessed=2 * rows * width,
            transcendentals=rows * hidden_units,
        ),
        name="experts_second",
    )(*flat, mask, *sums, held(w_gate), held(w_up), held(w_down))


def rest_kernel(rest, w_down, near, far):
    size = w_down.shape[1] // CHUNKS
    mine = near.shape[0]

    @pl.loop(0, CHUNKS)
    def _(n):
        columns = span(n, size)
        product = jnp.dot(rest[...], w_down[:, columns], preferred_element_type=jnp.float32)
        near[:, columns] = product[:mine].astype(jnp.bfloat16)
        far[:, columns] = product[mine:].astype(jnp.bfloat16)


def experts_rest(rest, w_down):
    rows, hidden_units = rest.shape
    width = w_down.shape[1]
    outs = jax.ShapeDtypeStruct((rows // 2, width), jnp.bfloat16)
    return pl.pallas_call(
        rest_kernel,
        out_shape=(outs, outs),
        in_specs=[vmem_spec()] * 2,
        out_specs=(vmem_spec(),) * 2,
        compiler_params=pltpu.CompilerParams(vmem_limit_bytes=24 << 20),
        cost_estimate=pl.CostEstimate(
            flops=2 * rows * width * hidden_units, bytes_accessed=2 * rows * width, transcendentals=0
        ),
        name="experts_rest",
    )(rest, held(w_down))


def moves(destination, replica_rows):
    slots = destination.shape[0]
    replicas = slots // replica_rows
    ids = jnp.arange(slots, dtype=jnp.int32)
    home = ids // replica_rows
    leaving = destination // replica_rows != home
    earlier = (home[:, None] == home[None, :]) & (ids[:, None] < ids[None, :])
    rank = jnp.sum(jnp.where(earlier & leaving[:, None], 1, 0), axis=0)
    box = jnp.where(leaving, home * MOVE_MAX + rank, -1)
    boxes = jnp.arange(replicas * MOVE_MAX, dtype=jnp.int32)
    to_box = (boxes[:, None] == box[None, :]).astype(jnp.bfloat16)
    lands = (ids[:, None] == destination[None, :]).astype(jnp.bfloat16)
    target = jnp.dot(to_box, lands, preferred_element_type=jnp.float32).astype(jnp.bfloat16)
    picker = lax.dot_general(
        target, to_box, (((1,), (1,)), ((), ())), preferred_element_type=jnp.float32
    ).astype(jnp.bfloat16)
    return to_box, picker


def migrate(packing, picker, latent_cache):
    replicas = lax.axis_size("dp")
    ep_count = lax.axis_size("ep")
    width = latent_cache.shape[1] // ep_count
    share = width // replicas
    own = lax.dynamic_slice_in_dim(latent_cache, lax.axis_index("ep") * width, width, axis=1)
    outbox = jnp.dot(packing, own, preferred_element_type=jnp.float32).astype(jnp.bfloat16)
    outbox = outbox.reshape(MOVE_MAX, replicas, share).transpose(1, 0, 2)
    met = lax.all_to_all(outbox, "dp", split_axis=0, concat_axis=0)
    sorted_rows = jnp.dot(
        picker, met.reshape(replicas * MOVE_MAX, share), preferred_element_type=jnp.float32
    ).astype(jnp.bfloat16)
    taken = lax.all_to_all(
        sorted_rows.reshape(replicas, MOVE_MAX, share), "dp", split_axis=0, concat_axis=0
    )
    part = taken.transpose(1, 0, 2).reshape(MOVE_MAX, width)
    return lax.all_gather(part, "ep", axis=1, tiled=True)


def all_sets(pieces):
    sets = [pieces]
    for bit in bits_of("ep"):
        sets = sets + [tuple(flip(piece, "ep", bit) for piece in one) for one in sets]
    return sets


def dp_bits():
    inner_x, inner_y, *outer = bits_of("dp")
    return inner_x, inner_y, outer[::-1]


def plus(*terms):
    return sum(term.astype(jnp.float32) for term in terms)


def narrow(x):
    return x.astype(jnp.bfloat16)


def ep_sums(near, far):
    bits = bits_of("ep")[::-1]
    for bit in bits:
        came = flip(far, "ep", bit)
        if bit != bits[-1]:
            near, far = jnp.split(narrow(plus(near, came)), 2, axis=0)
    return near, came


def scatter_sums(corner, rest):
    inner_x, inner_y, outer = dp_bits()
    half = corner[0].shape[1] // 2
    diagonal = narrow(plus(*ep_sums(*corner)))
    low = flip(diagonal[:, :half], "dp", inner_x)
    high = flip(diagonal[:, half:], "dp", inner_y)
    own, to_x, to_y = zip(*(jnp.split(term, 3, axis=0) for term in ep_sums(*rest)))
    to_x, to_y = plus(*to_x), plus(*to_y)
    to_x = narrow(jnp.concatenate([to_x[:, :half], to_x[:, half:] + plus(high)], axis=1))
    to_y = narrow(jnp.concatenate([to_y[:, :half] + plus(low), to_y[:, half:]], axis=1))
    from_x = flip(to_x, "dp", inner_x)
    from_y = flip(to_y, "dp", inner_y)
    total = plus(*own, from_x, from_y)
    for bit in outer[::-1]:
        mine, other = jnp.split(total, 2, axis=0)
        total = mine + plus(flip(narrow(other), "dp", bit))
    return total


def head_sums(part):
    if lax.axis_size("ep") != 2:
        return lax.psum_scatter(part, "ep", scatter_dimension=0, tiled=True)
    rows = part.shape[0] // 2
    own = lax.axis_index("ep")
    mine = lax.dynamic_slice_in_dim(part, own * rows, rows)
    other = lax.dynamic_slice_in_dim(part, (1 - own) * rows, rows)
    return mine + flip(other, "ep", 1)


def three_terms(x):
    terms = []
    for _ in range(3):
        term = lax.reduce_precision(x, 8, 7)
        terms.append(narrow(term))
        x = x - term
    return terms


def per_device(
    residual,
    queries,
    latent_cache,
    lengths,
    destination,
    w_uv,
    w_o,
    norm_gain,
    experts,
    gate_weights,
    w_gate,
    w_up,
    w_down,
):
    w_uv, w_o, w_gate, w_up, w_down = (
        pltpu.with_memory_space_constraint(w, pltpu.HBM) for w in (w_uv, w_o, w_gate, w_up, w_down)
    )
    replica_rows = latent_cache.shape[0]
    replicas = destination.shape[0] // replica_rows
    own_replica = lax.axis_index("dp")
    to_box, picker = moves(destination, replica_rows)
    packing = lax.dynamic_slice(
        to_box, (own_replica * MOVE_MAX, own_replica * replica_rows), (MOVE_MAX, replica_rows)
    )
    arrivals = migrate(packing, picker, latent_cache)
    boxes = jnp.arange(1, MOVE_MAX + 1, dtype=jnp.float32)[:, None]
    moved = jnp.sum(packing.astype(jnp.float32) * boxes, axis=0).astype(jnp.int32) - 1
    heads_dev = w_uv.shape[0]
    query_rows = queries.reshape(replica_rows, heads_dev, KV)
    cached = latent_cache.reshape(replica_rows, CTX, KV)
    arrived = arrivals.reshape(MOVE_MAX, CTX, KV)
    width = residual.shape[1]
    half, size = width // 2, width // CHUNKS
    tokens = residual.astype(jnp.float32)

    part, values = attention_and_first(
        moved, lengths, query_rows, cached, arrived, w_uv, w_o, half
    )
    hidden_a = tokens[:, :half] + head_sums(part)
    rows_a = narrow(hidden_a * norm_gain[None, :half])
    values, rows_a = lax.optimization_barrier((values, rows_a))
    inner_x, inner_y, outer = dp_bits()
    early = half * 2 // 5 // 128 * 128
    parts_b = [more_columns(values, w_o, half, early)]
    came, parts_b = lax.optimization_barrier((flip(rows_a, "dp", outer[0]), parts_b))
    held_a = jnp.concatenate([rows_a, came], axis=0)
    values, held_a = lax.optimization_barrier((values, held_a))
    parts_b.append(more_columns(values, w_o, half + early, half - early))
    for bit in outer[1:]:
        held_a = jnp.concatenate([held_a, flip(held_a, "dp", bit)], axis=0)
    parts_b, held_a = lax.optimization_barrier((parts_b, held_a))
    x_a = flip(held_a, "dp", inner_x)
    y_a = flip(held_a, "dp", inner_y)

    hidden_b = tokens[:, half:] + head_sums(jnp.concatenate(parts_b, axis=1))
    squares = jnp.sum(hidden_a * hidden_a, axis=1, keepdims=True) + jnp.sum(
        hidden_b * hidden_b, axis=1, keepdims=True
    )
    factor = lax.rsqrt(squares / width + norm_eps)
    expert_ids = jnp.arange(replicas, dtype=jnp.int32)
    matches = experts[:, :, None] == expert_ids[None, None, :]
    gate_sum = jnp.sum(jnp.where(matches, gate_weights[:, :, None], 0.0), axis=1)
    terms = three_terms(gate_sum) + three_terms(factor)
    terms.append(jnp.zeros((tokens.shape[0], GATE_COLS - 3 * replicas - 3), jnp.bfloat16))
    rows_b = jnp.concatenate([narrow(hidden_b * norm_gain[None, half:])] + terms, axis=1)
    held_b = jnp.concatenate([rows_b, flip(rows_b, "dp", outer[0])], axis=0)
    held_b, x_a, y_a = lax.optimization_barrier((held_b, x_a, y_a))
    low_a = flip(y_a[:, :size], "dp", inner_x)
    high_a = flip(x_a[:, size:], "dp", inner_y)
    for bit in outer[1:]:
        held_b = jnp.concatenate([held_b, flip(held_b, "dp", bit)], axis=0)
    columns = jnp.arange(GATE_COLS, dtype=jnp.int32)
    gate_mask = (columns < 3 * replicas) & (columns % replicas == own_replica)
    factor_mask = (columns >= 3 * replicas) & (columns < 3 * replicas + 3)
    mask = jnp.stack([gate_mask, factor_mask]).astype(jnp.float32)
    held_b, low_a, high_a, mask = lax.optimization_barrier((held_b, low_a, high_a, mask))
    x_b = flip(held_b, "dp", inner_x)
    y_b = flip(held_b, "dp", inner_y)
    gate_held, up_held, down_held, mask = hold_weights(mask, w_gate, w_up, w_down)
    low_a, high_a, mask = lax.optimization_barrier((low_a, high_a, mask))
    sets_a = all_sets((held_a, x_a, y_a, low_a, high_a))
    x_b, y_b, sets_a = lax.optimization_barrier((x_b, y_b, sets_a))
    low_b = flip(y_b[:, :size], "dp", inner_x)
    high_b = flip(x_b[:, size:], "dp", inner_y)
    sums = experts_first(sets_a, w_gate, w_up)
    low_b, high_b, sums = lax.optimization_barrier((low_b, high_b, sums))
    sets_b = all_sets((held_b, x_b, y_b, low_b, high_b))
    near, far, rest = experts_second(sets_b, mask, sums, gate_held, up_held, down_held)
    mixture = scatter_sums((near, far), experts_rest(rest, down_held))
    hidden = jnp.concatenate([hidden_a, hidden_b], axis=1)
    layer_out = (hidden + mixture).astype(jnp.bfloat16)
    return (layer_out, arrivals)


def solution(mesh):
    in_specs = (
        P(("dp", "ep"), None),
        P("dp", "ep"),
        P("dp", None),
        P("dp"),
        P(),
        P("ep", None, None),
        P("ep", None),
        P(),
        P(("dp", "ep"), None),
        P(("dp", "ep"), None),
        P("dp", None, "ep"),
        P("dp", None, "ep"),
        P("dp", "ep", None),
    )
    out_specs = (P(("dp", "ep"), None), P("dp", None))
    return jax.shard_map(
        per_device, mesh=mesh, in_specs=in_specs, out_specs=out_specs, check_vma=False
    )
```

```python
import functools

import jax
import jax.numpy as jnp
from jax import lax
from jax.experimental import pallas as pl
from jax.experimental.pallas import tpu as pltpu
from jax.sharding import PartitionSpec as P

LAT = 512
KV = 576
V_DIM = 128
MOVE_MAX = 4
CTX = 64
GATE_COLS = 128


score_scale = 192.0 ** (-0.5)
norm_eps = 1e-06


def flip(x, axis, bit):
    pairs = [(i, i ^ bit) for i in range(lax.axis_size(axis))]
    return lax.ppermute(x, axis, pairs)


def bits_of(axis):
    size = lax.axis_size(axis)
    return [1 << b for b in range(size.bit_length() - 1)]


CHUNKS = 4
IN_FLIGHT = 10 << 20


def vmem_spec():
    return pl.BlockSpec(memory_space=pltpu.VMEM)


def hbm_spec():
    return pl.BlockSpec(memory_space=pltpu.HBM)


def span(n, size):
    return pl.ds(pl.multiple_of(n * size, size), size)


def attention_kernel(
    moved, lengths, queries, cached, arrived, w_uv, w_o, part, values,
    keys, context, uv_buf, o_buf, uv_sems, o_sems,
):
    requests, heads, _ = queries.shape
    latent, dim = w_uv.shape[1:]
    groups = uv_sems.shape[0]
    step = heads // groups
    chunks, depth, width = o_buf.shape

    def copy_uv(g):
        own = pl.ds(g * step, step)
        return pltpu.make_async_copy(w_uv.at[own], uv_buf.at[own], uv_sems.at[g])

    def copy_o(n):
        rows = pl.ds(n * depth, depth)
        return pltpu.make_async_copy(w_o.at[rows, pl.ds(0, width)], o_buf.at[n], o_sems.at[n])

    for g in range(groups):
        copy_uv(g).start()
    ahead = min(chunks, max(2, 2 * IN_FLIGHT // (2 * depth * width)))
    for n in range(ahead):
        copy_o(n).start()
    for i in range(requests):
        row = moved[i]
        keys[i] = jnp.where(row >= 0, arrived[jnp.maximum(row, 0)], cached[i])
    scores, limits = [], []
    for i in range(requests):
        score = lax.dot_general(
            queries[i], keys[i], (((1,), (1,)), ((), ())), preferred_element_type=jnp.float32
        )
        scores.append(score)
        limits.append(jnp.full(score.shape, lengths[i], jnp.int32))
    scores = jnp.concatenate(scores, axis=0) * score_scale
    in_range = lax.broadcasted_iota(jnp.int32, scores.shape, 1) < jnp.concatenate(limits, axis=0)
    scores = jnp.where(in_range, scores, -jnp.inf)
    row_max = jnp.max(scores, axis=1, keepdims=True)
    weights = jnp.where(in_range, jnp.exp(scores - row_max), 0.0)
    probs = (weights / jnp.sum(weights, axis=1, keepdims=True)).astype(jnp.bfloat16)
    for i in range(requests):
        context[:, i, :] = jnp.dot(
            probs[i * heads : (i + 1) * heads],
            keys[i, :, :latent],
            preferred_element_type=jnp.float32,
        )
    for g in range(groups):
        copy_uv(g).wait()
        for h in range(g * step, (g + 1) * step):
            values[:, h * dim : (h + 1) * dim] = jnp.dot(
                context[h].astype(jnp.bfloat16), uv_buf[h], preferred_element_type=jnp.float32
            ).astype(jnp.bfloat16)
    for n in range(chunks):
        copy_o(n).wait()
        if n + ahead < chunks:
            copy_o(n + ahead).start()
        product = jnp.dot(
            values[:, n * depth : (n + 1) * depth], o_buf[n], preferred_element_type=jnp.float32
        )
        if n == 0:
            part[...] = product
        else:
            part[...] += product


def attention_and_first(moved, lengths, queries, cached, arrived, w_uv, w_o, width):
    requests, heads, key_width = queries.shape
    latent = w_uv.shape[1]
    depth = w_o.shape[0]
    chunks = 8
    groups = 4 if heads % 4 == 0 else 1
    smem = pl.BlockSpec(memory_space=pltpu.SMEM)
    return pl.pallas_call(
        attention_kernel,
        out_shape=(
            jax.ShapeDtypeStruct((requests, width), jnp.float32),
            jax.ShapeDtypeStruct((requests, depth), jnp.bfloat16),
        ),
        in_specs=[smem, smem] + [vmem_spec()] * 3 + [hbm_spec()] * 2,
        out_specs=(vmem_spec(), vmem_spec()),
        scratch_shapes=[
            pltpu.VMEM(cached.shape, jnp.bfloat16),
            pltpu.VMEM((heads, requests, latent), jnp.float32),
            pltpu.VMEM(w_uv.shape, jnp.bfloat16),
            pltpu.VMEM((chunks, depth // chunks, width), jnp.bfloat16),
            pltpu.SemaphoreType.DMA((groups,)),
            pltpu.SemaphoreType.DMA((chunks,)),
        ],
        compiler_params=pltpu.CompilerParams(vmem_limit_bytes=48 << 20),
        cost_estimate=pl.CostEstimate(
            flops=2 * requests * depth * (width + latent),
            bytes_accessed=2 * depth * (width + latent),
            transcendentals=requests * heads * CTX,
        ),
        name="attention_and_first",
    )(moved, lengths, queries, cached, arrived, w_uv, w_o)


def columns_kernel(start, values, w_o, part, o_buf, o_sems):
    chunks, depth, width = o_buf.shape

    def copy_o(n):
        rows = pl.ds(n * depth, depth)
        return pltpu.make_async_copy(w_o.at[rows, pl.ds(start, width)], o_buf.at[n], o_sems.at[n])

    ahead = min(chunks, max(2, IN_FLIGHT // (2 * depth * width)))
    for n in range(ahead):
        copy_o(n).start()
    for n in range(chunks):
        copy_o(n).wait()
        if n + ahead < chunks:
            copy_o(n + ahead).start()
        product = jnp.dot(
            values[:, n * depth : (n + 1) * depth], o_buf[n], preferred_element_type=jnp.float32
        )
        if n == 0:
            part[...] = product
        else:
            part[...] += product


def more_columns(values, w_o, start, width):
    rows, depth = values.shape
    chunks = 8
    return pl.pallas_call(
        functools.partial(columns_kernel, start),
        out_shape=jax.ShapeDtypeStruct((rows, width), jnp.float32),
        in_specs=[vmem_spec(), hbm_spec()],
        out_specs=vmem_spec(),
        scratch_shapes=[
            pltpu.VMEM((chunks, depth // chunks, width), jnp.bfloat16),
            pltpu.SemaphoreType.DMA((chunks,)),
        ],
        compiler_params=pltpu.CompilerParams(vmem_limit_bytes=24 << 20),
        cost_estimate=pl.CostEstimate(
            flops=2 * rows * depth * width, bytes_accessed=2 * depth * width, transcendentals=0
        ),
        name="more_columns",
    )(values, w_o)


def first_kernel(piece_count, *refs):
    pieces, refs = refs[:piece_count], refs[piece_count:]
    w_gate, w_up, gate_acc, up_acc, gate_buf, up_buf, sems = refs
    chunks, size, _ = gate_buf.shape

    def copies_in(n):
        return (
            pltpu.make_async_copy(w_gate.at[0, span(n, size)], gate_buf.at[n], sems.at[0, n]),
            pltpu.make_async_copy(w_up.at[0, span(n, size)], up_buf.at[n], sems.at[1, n]),
        )

    for n in range(chunks):
        for copy in copies_in(n):
            copy.start()
    for n in range(chunks):
        columns = slice(n * size, (n + 1) * size)
        rows = jnp.concatenate([ref[:, columns] for ref in pieces], axis=0)
        for copy in copies_in(n):
            copy.wait()
        gate_part = jnp.dot(rows, gate_buf[n], preferred_element_type=jnp.float32)
        up_part = jnp.dot(rows, up_buf[n], preferred_element_type=jnp.float32)
        if n == 0:
            gate_acc[...] = gate_part
            up_acc[...] = up_part
        else:
            gate_acc[...] += gate_part
            up_acc[...] += up_part


def experts_first(sets, w_gate, w_up):
    width, hidden_units = w_gate.shape[1:]
    size = width // CHUNKS
    flat = [piece for pieces in sets for piece in pieces]
    rows = sum(piece.shape[0] for piece in flat)
    sums = jax.ShapeDtypeStruct((rows, hidden_units), jnp.float32)
    return pl.pallas_call(
        functools.partial(first_kernel, len(flat)),
        out_shape=(sums, sums),
        in_specs=[vmem_spec()] * len(flat) + [hbm_spec()] * 2,
        out_specs=(vmem_spec(), vmem_spec()),
        scratch_shapes=[
            pltpu.VMEM((CHUNKS // 2, size, hidden_units), jnp.bfloat16),
            pltpu.VMEM((CHUNKS // 2, size, hidden_units), jnp.bfloat16),
            pltpu.SemaphoreType.DMA((2, CHUNKS // 2)),
        ],
        compiler_params=pltpu.CompilerParams(vmem_limit_bytes=32 << 20),
        cost_estimate=pl.CostEstimate(
            flops=2 * rows * width * hidden_units,
            bytes_accessed=2 * width * hidden_units + rows * width,
            transcendentals=0,
        ),
        name="experts_first",
    )(*flat, w_gate, w_up)


def hold_kernel(after, w_gate, w_up, w_down, gate, up, down, done, sems):
    half = gate.shape[0]
    parts = sems.shape[1]

    def copies(n):
        size = half // parts
        rows = pl.ds(n * size, size)
        later = pl.ds(half + n * size, size)
        units = pl.ds(n * (down.shape[0] // parts), down.shape[0] // parts)
        return (
            pltpu.make_async_copy(w_gate.at[0, later], gate.at[rows], sems.at[0, n]),
            pltpu.make_async_copy(w_up.at[0, later], up.at[rows], sems.at[1, n]),
            pltpu.make_async_copy(w_down.at[0, units], down.at[units], sems.at[2, n]),
        )

    for n in range(parts):
        for copy in copies(n):
            copy.start()
    done[...] = after[...]
    for n in range(parts):
        for copy in copies(n):
            copy.wait()


def hold_weights(after, w_gate, w_up, w_down):
    width, hidden_units = w_gate.shape[1:]
    half = width // 2
    return pl.pallas_call(
        hold_kernel,
        out_shape=(
            pltpu.VMEM((half, hidden_units), jnp.bfloat16),
            pltpu.VMEM((half, hidden_units), jnp.bfloat16),
            pltpu.VMEM((hidden_units, width), jnp.bfloat16),
            jax.ShapeDtypeStruct(after.shape, after.dtype),
        ),
        in_specs=[vmem_spec()] + [hbm_spec()] * 3,
        out_specs=(vmem_spec(),) * 4,
        scratch_shapes=[pltpu.SemaphoreType.DMA((3, 2))],
        compiler_params=pltpu.CompilerParams(vmem_limit_bytes=4 << 20),
        cost_estimate=pl.CostEstimate(
            flops=0, bytes_accessed=4 * width * hidden_units, transcendentals=0
        ),
        name="hold_weights",
    )(after, w_gate, w_up, w_down)


def held(array):
    return pltpu.with_memory_space_constraint(array, pltpu.VMEM)


def second_kernel(set_count, *refs):
    pieces, refs = refs[: 4 * set_count], refs[4 * set_count :]
    mask, gate_first, up_first, w_gate, w_up, w_down = refs[:6]
    near, far, rest, gate_acc, up_acc, act = refs[6:]
    half = w_gate.shape[0]
    size = half // 2
    line = near.shape[0] * 2 // set_count
    terms = jnp.concatenate([ref[:, half:] for ref in pieces], axis=0).astype(jnp.float32)
    gates = jnp.sum(terms * mask[0:1], axis=1, keepdims=True)
    factors = jnp.sum(terms * mask[1:2], axis=1, keepdims=True)
    for n in range(2):
        depth = slice(n * size, (n + 1) * size)
        rows = jnp.concatenate([ref[:, depth] for ref in pieces], axis=0)
        before = (gate_first, up_first) if n == 0 else (gate_acc, up_acc)
        gate_acc[...] = before[0][...] + jnp.dot(
            rows, w_gate[depth], preferred_element_type=jnp.float32
        )
        up_acc[...] = before[1][...] + jnp.dot(
            rows, w_up[depth], preferred_element_type=jnp.float32
        )
    gated = gate_acc[...] * factors
    raised = up_acc[...] * factors
    act[...] = (gated / (1.0 + jnp.exp(-gated)) * raised * gates).astype(jnp.bfloat16)
    corners = []
    for n in range(set_count):
        rest[n * 3 * line : (n + 1) * 3 * line] = act[n * 4 * line : (n * 4 + 3) * line]
        corners.append(act[(n * 4 + 3) * line : (n + 1) * 4 * line])
    corner = jnp.concatenate(corners, axis=0)
    mine = near.shape[0]

    @pl.loop(0, CHUNKS)
    def _(n):
        columns = span(n, size)
        product = jnp.dot(corner, w_down[:, columns], preferred_element_type=jnp.float32)
        near[:, columns] = product[:mine].astype(jnp.bfloat16)
        far[:, columns] = product[mine:].astype(jnp.bfloat16)


def experts_second(sets, mask, sums, w_gate, w_up, w_down):
    hidden_units, width = w_down.shape
    rows = sums[0].shape[0]
    flat = [piece for pieces in sets for piece in pieces]
    corner = jax.ShapeDtypeStruct((rows // 8, width), jnp.bfloat16)
    return pl.pallas_call(
        functools.partial(second_kernel, len(sets)),
        out_shape=(
            corner,
            corner,
            jax.ShapeDtypeStruct((rows // 4 * 3, hidden_units), jnp.bfloat16),
        ),
        in_specs=[vmem_spec()] * (len(flat) + 6),
        out_specs=(vmem_spec(),) * 3,
        scratch_shapes=[
            pltpu.VMEM((rows, hidden_units), jnp.float32),
            pltpu.VMEM((rows, hidden_units), jnp.float32),
            pltpu.VMEM((rows, hidden_units), jnp.bfloat16),
        ],
        compiler_params=pltpu.CompilerParams(vmem_limit_bytes=24 << 20),
        cost_estimate=pl.CostEstimate(
            flops=3 * rows * width * hidden_units,
            bytes_accessed=2 * rows * width,
            transcendentals=rows * hidden_units,
        ),
        name="experts_second",
    )(*flat, mask, *sums, held(w_gate), held(w_up), held(w_down))


def rest_kernel(rest, w_down, near, far):
    size = w_down.shape[1] // CHUNKS
    mine = near.shape[0]

    @pl.loop(0, CHUNKS)
    def _(n):
        columns = span(n, size)
        product = jnp.dot(rest[...], w_down[:, columns], preferred_element_type=jnp.float32)
        near[:, columns] = product[:mine].astype(jnp.bfloat16)
        far[:, columns] = product[mine:].astype(jnp.bfloat16)


def experts_rest(rest, w_down):
    rows, hidden_units = rest.shape
    width = w_down.shape[1]
    outs = jax.ShapeDtypeStruct((rows // 2, width), jnp.bfloat16)
    return pl.pallas_call(
        rest_kernel,
        out_shape=(outs, outs),
        in_specs=[vmem_spec()] * 2,
        out_specs=(vmem_spec(),) * 2,
        compiler_params=pltpu.CompilerParams(vmem_limit_bytes=24 << 20),
        cost_estimate=pl.CostEstimate(
            flops=2 * rows * width * hidden_units, bytes_accessed=2 * rows * width, transcendentals=0
        ),
        name="experts_rest",
    )(rest, held(w_down))


def moves(destination, replica_rows):
    slots = destination.shape[0]
    replicas = slots // replica_rows
    ids = jnp.arange(slots, dtype=jnp.int32)
    home = ids // replica_rows
    leaving = destination // replica_rows != home
    earlier = (home[:, None] == home[None, :]) & (ids[:, None] < ids[None, :])
    rank = jnp.sum(jnp.where(earlier & leaving[:, None], 1, 0), axis=0)
    box = jnp.where(leaving, home * MOVE_MAX + rank, -1)
    boxes = jnp.arange(replicas * MOVE_MAX, dtype=jnp.int32)
    to_box = (boxes[:, None] == box[None, :]).astype(jnp.bfloat16)
    lands = (ids[:, None] == destination[None, :]).astype(jnp.bfloat16)
    target = jnp.dot(to_box, lands, preferred_element_type=jnp.float32).astype(jnp.bfloat16)
    picker = lax.dot_general(
        target, to_box, (((1,), (1,)), ((), ())), preferred_element_type=jnp.float32
    ).astype(jnp.bfloat16)
    return to_box, picker


def migrate(packing, picker, latent_cache):
    replicas = lax.axis_size("dp")
    ep_count = lax.axis_size("ep")
    width = latent_cache.shape[1] // ep_count
    share = width // replicas
    own = lax.dynamic_slice_in_dim(latent_cache, lax.axis_index("ep") * width, width, axis=1)
    outbox = jnp.dot(packing, own, preferred_element_type=jnp.float32).astype(jnp.bfloat16)
    outbox = outbox.reshape(MOVE_MAX, replicas, share).transpose(1, 0, 2)
    met = lax.all_to_all(outbox, "dp", split_axis=0, concat_axis=0)
    sorted_rows = jnp.dot(
        picker, met.reshape(replicas * MOVE_MAX, share), preferred_element_type=jnp.float32
    ).astype(jnp.bfloat16)
    taken = lax.all_to_all(
        sorted_rows.reshape(replicas, MOVE_MAX, share), "dp", split_axis=0, concat_axis=0
    )
    part = taken.transpose(1, 0, 2).reshape(MOVE_MAX, width)
    return lax.all_gather(part, "ep", axis=1, tiled=True)


def all_sets(pieces):
    sets = [pieces]
    for bit in bits_of("ep"):
        sets = sets + [tuple(flip(piece, "ep", bit) for piece in one) for one in sets]
    return sets


def dp_bits():
    inner_x, inner_y, *outer = bits_of("dp")
    return inner_x, inner_y, outer[::-1]


def plus(*terms):
    return sum(term.astype(jnp.float32) for term in terms)


def narrow(x):
    return x.astype(jnp.bfloat16)


def ep_sums(near, far):
    bits = bits_of("ep")[::-1]
    for bit in bits:
        came = flip(far, "ep", bit)
        if bit != bits[-1]:
            near, far = jnp.split(narrow(plus(near, came)), 2, axis=0)
    return near, came


def scatter_sums(corner, rest):
    inner_x, inner_y, outer = dp_bits()
    half = corner[0].shape[1] // 2
    diagonal = narrow(plus(*ep_sums(*corner)))
    low = flip(diagonal[:, :half], "dp", inner_x)
    high = flip(diagonal[:, half:], "dp", inner_y)
    own, to_x, to_y = zip(*(jnp.split(term, 3, axis=0) for term in ep_sums(*rest)))
    to_x, to_y = plus(*to_x), plus(*to_y)
    to_x = narrow(jnp.concatenate([to_x[:, :half], to_x[:, half:] + plus(high)], axis=1))
    to_y = narrow(jnp.concatenate([to_y[:, :half] + plus(low), to_y[:, half:]], axis=1))
    from_x = flip(to_x, "dp", inner_x)
    from_y = flip(to_y, "dp", inner_y)
    total = plus(*own, from_x, from_y)
    for bit in outer[::-1]:
        mine, other = jnp.split(total, 2, axis=0)
        total = mine + plus(flip(narrow(other), "dp", bit))
    return total


def head_sums(part):
    if lax.axis_size("ep") != 2:
        return lax.psum_scatter(part, "ep", scatter_dimension=0, tiled=True)
    rows = part.shape[0] // 2
    own = lax.axis_index("ep")
    mine = lax.dynamic_slice_in_dim(part, own * rows, rows)
    other = lax.dynamic_slice_in_dim(part, (1 - own) * rows, rows)
    return mine + flip(other, "ep", 1)


def three_terms(x):
    terms = []
    for _ in range(3):
        term = lax.reduce_precision(x, 8, 7)
        terms.append(narrow(term))
        x = x - term
    return terms


def per_device(
    residual,
    queries,
    latent_cache,
    lengths,
    destination,
    w_uv,
    w_o,
    norm_gain,
    experts,
    gate_weights,
    w_gate,
    w_up,
    w_down,
):
    w_uv, w_o, w_gate, w_up, w_down = (
        pltpu.with_memory_space_constraint(w, pltpu.HBM) for w in (w_uv, w_o, w_gate, w_up, w_down)
    )
    replica_rows = latent_cache.shape[0]
    replicas = destination.shape[0] // replica_rows
    own_replica = lax.axis_index("dp")
    to_box, picker = moves(destination, replica_rows)
    packing = lax.dynamic_slice(
        to_box, (own_replica * MOVE_MAX, own_replica * replica_rows), (MOVE_MAX, replica_rows)
    )
    arrivals = migrate(packing, picker, latent_cache)
    boxes = jnp.arange(1, MOVE_MAX + 1, dtype=jnp.float32)[:, None]
    moved = jnp.sum(packing.astype(jnp.float32) * boxes, axis=0).astype(jnp.int32) - 1
    heads_dev = w_uv.shape[0]
    query_rows = queries.reshape(replica_rows, heads_dev, KV)
    cached = latent_cache.reshape(replica_rows, CTX, KV)
    arrived = arrivals.reshape(MOVE_MAX, CTX, KV)
    width = residual.shape[1]
    half = width // 2
    tokens = residual.astype(jnp.float32)

    part, values = attention_and_first(
        moved, lengths, query_rows, cached, arrived, w_uv, w_o, half
    )
    hidden_a = tokens[:, :half] + head_sums(part)
    rows_a = narrow(hidden_a * norm_gain[None, :half])
    values, rows_a = lax.optimization_barrier((values, rows_a))
    inner_x, inner_y, outer = dp_bits()
    third = half * 2 // 7 // 128 * 128
    parts_b = [more_columns(values, w_o, half, third)]
    came, parts_b = lax.optimization_barrier((flip(rows_a, "dp", outer[0]), parts_b))
    held_a = jnp.concatenate([rows_a, came], axis=0)
    values, held_a = lax.optimization_barrier((values, held_a))
    parts_b.append(more_columns(values, w_o, half + third, third))
    for bit in outer[1:]:
        held_a = jnp.concatenate([held_a, flip(held_a, "dp", bit)], axis=0)
    values, parts_b, held_a = lax.optimization_barrier((values, parts_b, held_a))
    x_a = flip(held_a, "dp", inner_x)
    y_a = flip(held_a, "dp", inner_y)
    parts_b.append(more_columns(values, w_o, half + 2 * third, half - 2 * third))
    parts_b, x_a, y_a = lax.optimization_barrier((parts_b, x_a, y_a))

    hidden_b = tokens[:, half:] + head_sums(jnp.concatenate(parts_b, axis=1))
    squares = jnp.sum(hidden_a * hidden_a, axis=1, keepdims=True) + jnp.sum(
        hidden_b * hidden_b, axis=1, keepdims=True
    )
    factor = lax.rsqrt(squares / width + norm_eps)
    expert_ids = jnp.arange(replicas, dtype=jnp.int32)
    matches = experts[:, :, None] == expert_ids[None, None, :]
    gate_sum = jnp.sum(jnp.where(matches, gate_weights[:, :, None], 0.0), axis=1)
    terms = three_terms(gate_sum) + three_terms(factor)
    terms.append(jnp.zeros((tokens.shape[0], GATE_COLS - 3 * replicas - 3), jnp.bfloat16))
    rows_b = jnp.concatenate([narrow(hidden_b * norm_gain[None, half:])] + terms, axis=1)
    columns = jnp.arange(GATE_COLS, dtype=jnp.int32)
    gate_mask = (columns < 3 * replicas) & (columns % replicas == own_replica)
    factor_mask = (columns >= 3 * replicas) & (columns < 3 * replicas + 3)
    mask = jnp.stack([gate_mask, factor_mask]).astype(jnp.float32)
    corner_a = flip(y_a, "dp", inner_x)
    rows_b, mask = lax.optimization_barrier((rows_b, mask))
    came = flip(rows_b, "dp", outer[0])
    gate_held, up_held, down_held, mask = hold_weights(mask, w_gate, w_up, w_down)
    came, corner_a, mask = lax.optimization_barrier((came, corner_a, mask))
    held_b = jnp.concatenate([rows_b, came], axis=0)
    for bit in outer[1:]:
        held_b = jnp.concatenate([held_b, flip(held_b, "dp", bit)], axis=0)
    sets_a = all_sets((held_a, x_a, y_a, corner_a))
    x_b = flip(held_b, "dp", inner_x)
    y_b = flip(held_b, "dp", inner_y)
    sums = experts_first(sets_a, w_gate, w_up)
    x_b, y_b, sums = lax.optimization_barrier((x_b, y_b, sums))
    sets_b = all_sets((held_b, x_b, y_b, flip(x_b, "dp", inner_y)))
    near, far, rest = experts_second(sets_b, mask, sums, gate_held, up_held, down_held)
    mixture = scatter_sums((near, far), experts_rest(rest, down_held))
    hidden = jnp.concatenate([hidden_a, hidden_b], axis=1)
    layer_out = (hidden + mixture).astype(jnp.bfloat16)
    return (layer_out, arrivals)


def solution(mesh):
    in_specs = (
        P(("dp", "ep"), None),
        P("dp", "ep"),
        P("dp", None),
        P("dp"),
        P(),
        P("ep", None, None),
        P("ep", None),
        P(),
        P(("dp", "ep"), None),
        P(("dp", "ep"), None),
        P("dp", None, "ep"),
        P("dp", None, "ep"),
        P("dp", "ep", None),
    )
    out_specs = (P(("dp", "ep"), None), P("dp", None))
    return jax.shard_map(
        per_device, mesh=mesh, in_specs=in_specs, out_specs=out_specs, check_vma=False
    )
```

```python
import functools

import jax
import jax.numpy as jnp
from jax import lax
from jax.experimental import pallas as pl
from jax.experimental.pallas import tpu as pltpu
from jax.sharding import PartitionSpec as P

LAT = 512
KV = 576
V_DIM = 128
MOVE_MAX = 4
CTX = 64
GATE_COLS = 128


score_scale = 192.0 ** (-0.5)
norm_eps = 1e-06


def flip(x, axis, bit):
    pairs = [(i, i ^ bit) for i in range(lax.axis_size(axis))]
    return lax.ppermute(x, axis, pairs)


def bits_of(axis):
    size = lax.axis_size(axis)
    return [1 << b for b in range(size.bit_length() - 1)]


CHUNKS = 4
OUTER_FIRST = 0.125
IN_FLIGHT = 10 << 20


def vmem_spec():
    return pl.BlockSpec(memory_space=pltpu.VMEM)


def hbm_spec():
    return pl.BlockSpec(memory_space=pltpu.HBM)


def span(n, size):
    return pl.ds(pl.multiple_of(n * size, size), size)


def attention_kernel(
    moved, lengths, queries, cached, arrived, w_uv, w_o, part, values,
    keys, context, uv_buf, o_buf, uv_sems, o_sems,
):
    requests, heads, _ = queries.shape
    latent, dim = w_uv.shape[1:]
    groups = uv_sems.shape[0]
    step = heads // groups
    chunks, depth, width = o_buf.shape

    def copy_uv(g):
        own = pl.ds(g * step, step)
        return pltpu.make_async_copy(w_uv.at[own], uv_buf.at[own], uv_sems.at[g])

    def copy_o(n):
        rows = pl.ds(n * depth, depth)
        return pltpu.make_async_copy(w_o.at[rows, pl.ds(0, width)], o_buf.at[n], o_sems.at[n])

    for g in range(groups):
        copy_uv(g).start()
    ahead = min(chunks, max(2, 2 * IN_FLIGHT // (2 * depth * width)))
    for n in range(ahead):
        copy_o(n).start()
    for i in range(requests):
        row = moved[i]
        keys[i] = jnp.where(row >= 0, arrived[jnp.maximum(row, 0)], cached[i])
    scores, limits = [], []
    for i in range(requests):
        score = lax.dot_general(
            queries[i], keys[i], (((1,), (1,)), ((), ())), preferred_element_type=jnp.float32
        )
        scores.append(score)
        limits.append(jnp.full(score.shape, lengths[i], jnp.int32))
    scores = jnp.concatenate(scores, axis=0) * score_scale
    in_range = lax.broadcasted_iota(jnp.int32, scores.shape, 1) < jnp.concatenate(limits, axis=0)
    scores = jnp.where(in_range, scores, -jnp.inf)
    row_max = jnp.max(scores, axis=1, keepdims=True)
    weights = jnp.where(in_range, jnp.exp(scores - row_max), 0.0)
    probs = (weights / jnp.sum(weights, axis=1, keepdims=True)).astype(jnp.bfloat16)
    for i in range(requests):
        context[:, i, :] = jnp.dot(
            probs[i * heads : (i + 1) * heads],
            keys[i, :, :latent],
            preferred_element_type=jnp.float32,
        )
    for g in range(groups):
        copy_uv(g).wait()
        for h in range(g * step, (g + 1) * step):
            values[:, h * dim : (h + 1) * dim] = jnp.dot(
                context[h].astype(jnp.bfloat16), uv_buf[h], preferred_element_type=jnp.float32
            ).astype(jnp.bfloat16)
    for n in range(chunks):
        copy_o(n).wait()
        if n + ahead < chunks:
            copy_o(n + ahead).start()
        product = jnp.dot(
            values[:, n * depth : (n + 1) * depth], o_buf[n], preferred_element_type=jnp.float32
        )
        if n == 0:
            part[...] = product
        else:
            part[...] += product


def attention_and_first(moved, lengths, queries, cached, arrived, w_uv, w_o, width):
    requests, heads, key_width = queries.shape
    latent = w_uv.shape[1]
    depth = w_o.shape[0]
    chunks = 8
    groups = 4 if heads % 4 == 0 else 1
    smem = pl.BlockSpec(memory_space=pltpu.SMEM)
    return pl.pallas_call(
        attention_kernel,
        out_shape=(
            jax.ShapeDtypeStruct((requests, width), jnp.float32),
            jax.ShapeDtypeStruct((requests, depth), jnp.bfloat16),
        ),
        in_specs=[smem, smem] + [vmem_spec()] * 3 + [hbm_spec()] * 2,
        out_specs=(vmem_spec(), vmem_spec()),
        scratch_shapes=[
            pltpu.VMEM(cached.shape, jnp.bfloat16),
            pltpu.VMEM((heads, requests, latent), jnp.float32),
            pltpu.VMEM(w_uv.shape, jnp.bfloat16),
            pltpu.VMEM((chunks, depth // chunks, width), jnp.bfloat16),
            pltpu.SemaphoreType.DMA((groups,)),
            pltpu.SemaphoreType.DMA((chunks,)),
        ],
        compiler_params=pltpu.CompilerParams(vmem_limit_bytes=48 << 20),
        cost_estimate=pl.CostEstimate(
            flops=2 * requests * depth * (width + latent),
            bytes_accessed=2 * depth * (width + latent),
            transcendentals=requests * heads * CTX,
        ),
        name="attention_and_first",
    )(moved, lengths, queries, cached, arrived, w_uv, w_o)


def columns_kernel(start, values, w_o, part, o_buf, o_sems):
    chunks, depth, width = o_buf.shape

    def copy_o(n):
        rows = pl.ds(n * depth, depth)
        return pltpu.make_async_copy(w_o.at[rows, pl.ds(start, width)], o_buf.at[n], o_sems.at[n])

    ahead = min(chunks, max(2, IN_FLIGHT // (2 * depth * width)))
    for n in range(ahead):
        copy_o(n).start()
    for n in range(chunks):
        copy_o(n).wait()
        if n + ahead < chunks:
            copy_o(n + ahead).start()
        product = jnp.dot(
            values[:, n * depth : (n + 1) * depth], o_buf[n], preferred_element_type=jnp.float32
        )
        if n == 0:
            part[...] = product
        else:
            part[...] += product


def more_columns(values, w_o, start, width):
    rows, depth = values.shape
    chunks = 8
    return pl.pallas_call(
        functools.partial(columns_kernel, start),
        out_shape=jax.ShapeDtypeStruct((rows, width), jnp.float32),
        in_specs=[vmem_spec(), hbm_spec()],
        out_specs=vmem_spec(),
        scratch_shapes=[
            pltpu.VMEM((chunks, depth // chunks, width), jnp.bfloat16),
            pltpu.SemaphoreType.DMA((chunks,)),
        ],
        compiler_params=pltpu.CompilerParams(vmem_limit_bytes=24 << 20),
        cost_estimate=pl.CostEstimate(
            flops=2 * rows * depth * width, bytes_accessed=2 * depth * width, transcendentals=0
        ),
        name="more_columns",
    )(values, w_o)


def first_kernel(piece_count, *refs):
    pieces, refs = refs[:piece_count], refs[piece_count:]
    w_gate, w_up, gate_acc, up_acc, gate_buf, up_buf, sems = refs
    chunks, size, _ = gate_buf.shape

    def copies_in(n):
        return (
            pltpu.make_async_copy(w_gate.at[0, span(n, size)], gate_buf.at[n], sems.at[0, n]),
            pltpu.make_async_copy(w_up.at[0, span(n, size)], up_buf.at[n], sems.at[1, n]),
        )

    for n in range(chunks):
        for copy in copies_in(n):
            copy.start()
    for n in range(chunks):
        columns = slice(n * size, (n + 1) * size)
        rows = jnp.concatenate([ref[:, columns] for ref in pieces], axis=0)
        for copy in copies_in(n):
            copy.wait()
        gate_part = jnp.dot(rows, gate_buf[n], preferred_element_type=jnp.float32)
        up_part = jnp.dot(rows, up_buf[n], preferred_element_type=jnp.float32)
        if n == 0:
            gate_acc[...] = gate_part
            up_acc[...] = up_part
        else:
            gate_acc[...] += gate_part
            up_acc[...] += up_part


def experts_first(sets, w_gate, w_up):
    width, hidden_units = w_gate.shape[1:]
    size = width // CHUNKS
    flat = [piece for pieces in sets for piece in pieces]
    rows = sum(piece.shape[0] for piece in flat)
    sums = jax.ShapeDtypeStruct((rows, hidden_units), jnp.float32)
    return pl.pallas_call(
        functools.partial(first_kernel, len(flat)),
        out_shape=(sums, sums),
        in_specs=[vmem_spec()] * len(flat) + [hbm_spec()] * 2,
        out_specs=(vmem_spec(), vmem_spec()),
        scratch_shapes=[
            pltpu.VMEM((CHUNKS // 2, size, hidden_units), jnp.bfloat16),
            pltpu.VMEM((CHUNKS // 2, size, hidden_units), jnp.bfloat16),
            pltpu.SemaphoreType.DMA((2, CHUNKS // 2)),
        ],
        compiler_params=pltpu.CompilerParams(vmem_limit_bytes=32 << 20),
        cost_estimate=pl.CostEstimate(
            flops=2 * rows * width * hidden_units,
            bytes_accessed=2 * width * hidden_units + rows * width,
            transcendentals=0,
        ),
        name="experts_first",
    )(*flat, w_gate, w_up)


def hold_kernel(after, w_gate, w_up, w_down, gate, up, down, done, sems):
    half = gate.shape[0]
    parts = sems.shape[1]

    def copies(n):
        size = half // parts
        rows = pl.ds(n * size, size)
        later = pl.ds(half + n * size, size)
        units = pl.ds(n * (down.shape[0] // parts), down.shape[0] // parts)
        return (
            pltpu.make_async_copy(w_gate.at[0, later], gate.at[rows], sems.at[0, n]),
            pltpu.make_async_copy(w_up.at[0, later], up.at[rows], sems.at[1, n]),
            pltpu.make_async_copy(w_down.at[0, units], down.at[units], sems.at[2, n]),
        )

    for n in range(parts):
        for copy in copies(n):
            copy.start()
    done[...] = after[...]
    for n in range(parts):
        for copy in copies(n):
            copy.wait()


def hold_weights(after, w_gate, w_up, w_down):
    width, hidden_units = w_gate.shape[1:]
    half = width // 2
    return pl.pallas_call(
        hold_kernel,
        out_shape=(
            pltpu.VMEM((half, hidden_units), jnp.bfloat16),
            pltpu.VMEM((half, hidden_units), jnp.bfloat16),
            pltpu.VMEM((hidden_units, width), jnp.bfloat16),
            jax.ShapeDtypeStruct(after.shape, after.dtype),
        ),
        in_specs=[vmem_spec()] + [hbm_spec()] * 3,
        out_specs=(vmem_spec(),) * 4,
        scratch_shapes=[pltpu.SemaphoreType.DMA((3, 2))],
        compiler_params=pltpu.CompilerParams(vmem_limit_bytes=4 << 20),
        cost_estimate=pl.CostEstimate(
            flops=0, bytes_accessed=4 * width * hidden_units, transcendentals=0
        ),
        name="hold_weights",
    )(after, w_gate, w_up, w_down)


def held(array):
    return pltpu.with_memory_space_constraint(array, pltpu.VMEM)


def second_kernel(set_count, *refs):
    pieces, refs = refs[: 4 * set_count], refs[4 * set_count :]
    mask, gate_first, up_first, w_gate, w_up, w_down = refs[:6]
    near, far, rest, gate_acc, up_acc, act = refs[6:]
    half = w_gate.shape[0]
    size = half // 2
    line = near.shape[0] * 2 // set_count
    terms = jnp.concatenate([ref[:, half:] for ref in pieces], axis=0).astype(jnp.float32)
    gates = jnp.sum(terms * mask[0:1], axis=1, keepdims=True)
    factors = jnp.sum(terms * mask[1:2], axis=1, keepdims=True)
    for n in range(2):
        depth = slice(n * size, (n + 1) * size)
        rows = jnp.concatenate([ref[:, depth] for ref in pieces], axis=0)
        before = (gate_first, up_first) if n == 0 else (gate_acc, up_acc)
        gate_acc[...] = before[0][...] + jnp.dot(
            rows, w_gate[depth], preferred_element_type=jnp.float32
        )
        up_acc[...] = before[1][...] + jnp.dot(
            rows, w_up[depth], preferred_element_type=jnp.float32
        )
    gated = gate_acc[...] * factors
    raised = up_acc[...] * factors
    act[...] = (gated / (1.0 + jnp.exp(-gated)) * raised * gates).astype(jnp.bfloat16)
    corners = []
    for n in range(set_count):
        rest[n * 3 * line : (n + 1) * 3 * line] = act[n * 4 * line : (n * 4 + 3) * line]
        corners.append(act[(n * 4 + 3) * line : (n + 1) * 4 * line])
    corner = jnp.concatenate(corners, axis=0)
    mine = near.shape[0]

    @pl.loop(0, CHUNKS)
    def _(n):
        columns = span(n, size)
        product = jnp.dot(corner, w_down[:, columns], preferred_element_type=jnp.float32)
        near[:, columns] = product[:mine].astype(jnp.bfloat16)
        far[:, columns] = product[mine:].astype(jnp.bfloat16)


def experts_second(sets, mask, sums, w_gate, w_up, w_down):
    hidden_units, width = w_down.shape
    rows = sums[0].shape[0]
    flat = [piece for pieces in sets for piece in pieces]
    corner = jax.ShapeDtypeStruct((rows // 8, width), jnp.bfloat16)
    return pl.pallas_call(
        functools.partial(second_kernel, len(sets)),
        out_shape=(
            corner,
            corner,
            jax.ShapeDtypeStruct((rows // 4 * 3, hidden_units), jnp.bfloat16),
        ),
        in_specs=[vmem_spec()] * (len(flat) + 6),
        out_specs=(vmem_spec(),) * 3,
        scratch_shapes=[
            pltpu.VMEM((rows, hidden_units), jnp.float32),
            pltpu.VMEM((rows, hidden_units), jnp.float32),
            pltpu.VMEM((rows, hidden_units), jnp.bfloat16),
        ],
        compiler_params=pltpu.CompilerParams(vmem_limit_bytes=24 << 20),
        cost_estimate=pl.CostEstimate(
            flops=3 * rows * width * hidden_units,
            bytes_accessed=2 * rows * width,
            transcendentals=rows * hidden_units,
        ),
        name="experts_second",
    )(*flat, mask, *sums, held(w_gate), held(w_up), held(w_down))


def rest_kernel(rest, w_down, near, far):
    size = w_down.shape[1] // CHUNKS
    mine = near.shape[0]

    @pl.loop(0, CHUNKS)
    def _(n):
        columns = span(n, size)
        product = jnp.dot(rest[...], w_down[:, columns], preferred_element_type=jnp.float32)
        near[:, columns] = product[:mine].astype(jnp.bfloat16)
        far[:, columns] = product[mine:].astype(jnp.bfloat16)


def experts_rest(rest, w_down):
    rows, hidden_units = rest.shape
    width = w_down.shape[1]
    outs = jax.ShapeDtypeStruct((rows // 2, width), jnp.bfloat16)
    return pl.pallas_call(
        rest_kernel,
        out_shape=(outs, outs),
        in_specs=[vmem_spec()] * 2,
        out_specs=(vmem_spec(),) * 2,
        compiler_params=pltpu.CompilerParams(vmem_limit_bytes=24 << 20),
        cost_estimate=pl.CostEstimate(
            flops=2 * rows * width * hidden_units, bytes_accessed=2 * rows * width, transcendentals=0
        ),
        name="experts_rest",
    )(rest, held(w_down))


def moves(destination, replica_rows):
    slots = destination.shape[0]
    replicas = slots // replica_rows
    ids = jnp.arange(slots, dtype=jnp.int32)
    home = ids // replica_rows
    leaving = destination // replica_rows != home
    earlier = (home[:, None] == home[None, :]) & (ids[:, None] < ids[None, :])
    rank = jnp.sum(jnp.where(earlier & leaving[:, None], 1, 0), axis=0)
    box = jnp.where(leaving, home * MOVE_MAX + rank, -1)
    boxes = jnp.arange(replicas * MOVE_MAX, dtype=jnp.int32)
    to_box = (boxes[:, None] == box[None, :]).astype(jnp.bfloat16)
    lands = (ids[:, None] == destination[None, :]).astype(jnp.bfloat16)
    target = jnp.dot(to_box, lands, preferred_element_type=jnp.float32).astype(jnp.bfloat16)
    picker = lax.dot_general(
        target, to_box, (((1,), (1,)), ((), ())), preferred_element_type=jnp.float32
    ).astype(jnp.bfloat16)
    return picker


def migrate(packing, picker, latent_cache):
    replicas = lax.axis_size("dp")
    ep_count = lax.axis_size("ep")
    width = latent_cache.shape[1] // ep_count
    share = width // replicas
    own = lax.dynamic_slice_in_dim(latent_cache, lax.axis_index("ep") * width, width, axis=1)
    outbox = jnp.dot(packing, own, preferred_element_type=jnp.float32).astype(jnp.bfloat16)
    outbox = outbox.reshape(MOVE_MAX, replicas, share).transpose(1, 0, 2)
    met = lax.all_to_all(outbox, "dp", split_axis=0, concat_axis=0)
    sorted_rows = jnp.dot(
        picker, met.reshape(replicas * MOVE_MAX, share), preferred_element_type=jnp.float32
    ).astype(jnp.bfloat16)
    taken = lax.all_to_all(
        sorted_rows.reshape(replicas, MOVE_MAX, share), "dp", split_axis=0, concat_axis=0
    )
    part = taken.transpose(1, 0, 2).reshape(MOVE_MAX, width)
    return lax.all_gather(part, "ep", axis=1, tiled=True)


def all_sets(pieces):
    sets = [pieces]
    for bit in bits_of("ep"):
        sets = sets + [tuple(flip(piece, "ep", bit) for piece in one) for one in sets]
    return sets


def dp_bits():
    inner_x, inner_y, *outer = bits_of("dp")
    return inner_x, inner_y, outer[::-1]


def plus(*terms):
    return sum(term.astype(jnp.float32) for term in terms)


def narrow(x):
    return x.astype(jnp.bfloat16)


def ep_sums(near, far):
    bits = bits_of("ep")[::-1]
    for bit in bits:
        came = flip(far, "ep", bit)
        if bit != bits[-1]:
            near, far = jnp.split(narrow(plus(near, came)), 2, axis=0)
    return near, came


def outer_sums(lines, bits):
    for bit in bits:
        mine, other = jnp.split(lines, 2, axis=1)
        lines = mine + plus(flip(narrow(other), "dp", bit))
    return lines


def scatter_sums(corner, rest):
    inner_x, inner_y, outer = dp_bits()
    longest, *nearer = outer
    nearer = nearer[::-1]
    width = corner[0].shape[1]
    main = width - int(width * OUTER_FIRST) // 128 * 128
    half = main // 2 // 128 * 128
    corner = ep_sums(*corner)
    diagonal = narrow(plus(*(term[:, :main] for term in corner)))
    low = flip(diagonal[:, :half], "dp", inner_x)
    high = flip(diagonal[:, half:], "dp", inner_y)
    rest = [jnp.split(term, 3, axis=0) for term in ep_sums(*rest)]

    lines = [plus(*(term[n][:, main:] for term in rest)) for n in range(3)]
    lines.append(plus(*(term[:, main:] for term in corner)))
    lines = outer_sums(jnp.stack(lines), nearer)

    own, to_x, to_y = (plus(*(term[n][:, :main] for term in rest)) for n in range(3))
    to_x = narrow(jnp.concatenate([to_x[:, :half], to_x[:, half:] + plus(high)], axis=1))
    to_y = narrow(jnp.concatenate([to_y[:, :half] + plus(low), to_y[:, half:]], axis=1))
    from_x = flip(to_x, "dp", inner_x)
    from_y = flip(to_y, "dp", inner_y)
    first = outer_sums(plus(own, from_x, from_y)[None], nearer)[0]

    own, to_x, to_y, far = lines
    to_y = to_y + plus(flip(narrow(far), "dp", inner_x))
    from_x = flip(narrow(to_x), "dp", inner_x)
    from_y = flip(narrow(to_y), "dp", inner_y)
    last = own + plus(from_x, from_y)
    return outer_sums(jnp.concatenate([first, last], axis=1)[None], [longest])[0]


def head_sums(part):
    if lax.axis_size("ep") != 2:
        return lax.psum_scatter(part, "ep", scatter_dimension=0, tiled=True)
    rows = part.shape[0] // 2
    own = lax.axis_index("ep")
    mine = lax.dynamic_slice_in_dim(part, own * rows, rows)
    other = lax.dynamic_slice_in_dim(part, (1 - own) * rows, rows)
    return mine + flip(other, "ep", 1)


def three_terms(x):
    terms = []
    for _ in range(3):
        term = lax.reduce_precision(x, 8, 7)
        terms.append(narrow(term))
        x = x - term
    return terms


def per_device(
    residual,
    queries,
    latent_cache,
    lengths,
    destination,
    w_uv,
    w_o,
    norm_gain,
    experts,
    gate_weights,
    w_gate,
    w_up,
    w_down,
):
    w_uv, w_o, w_gate, w_up, w_down = (
        pltpu.with_memory_space_constraint(w, pltpu.HBM) for w in (w_uv, w_o, w_gate, w_up, w_down)
    )
    replica_rows = latent_cache.shape[0]
    replicas = destination.shape[0] // replica_rows
    own_replica = lax.axis_index("dp")
    picker = moves(destination, replica_rows)
    own_slots = lax.dynamic_slice_in_dim(destination, own_replica * replica_rows, replica_rows)
    leaving = own_slots // replica_rows != own_replica
    places = jnp.arange(replica_rows, dtype=jnp.int32)
    earlier = (places[:, None] < places[None, :]) & leaving[:, None]
    rank = jnp.sum(earlier.astype(jnp.int32), axis=0)
    box_ids = jnp.arange(MOVE_MAX, dtype=jnp.int32)
    packing = narrow((rank[None, :] == box_ids[:, None]) & leaving[None, :])
    arrivals = migrate(packing, picker, latent_cache)
    boxes = jnp.arange(1, MOVE_MAX + 1, dtype=jnp.float32)[:, None]
    moved = jnp.sum(packing.astype(jnp.float32) * boxes, axis=0).astype(jnp.int32) - 1
    heads_dev = w_uv.shape[0]
    query_rows = queries.reshape(replica_rows, heads_dev, KV)
    cached = latent_cache.reshape(replica_rows, CTX, KV)
    arrived = arrivals.reshape(MOVE_MAX, CTX, KV)
    width = residual.shape[1]
    half = width // 2
    tokens = residual.astype(jnp.float32)

    part, values = attention_and_first(
        moved, lengths, query_rows, cached, arrived, w_uv, w_o, half
    )
    hidden_a = tokens[:, :half] + head_sums(part)
    rows_a = narrow(hidden_a * norm_gain[None, :half])
    values, rows_a = lax.optimization_barrier((values, rows_a))
    inner_x, inner_y, outer = dp_bits()
    third = half * 2 // 7 // 128 * 128
    parts_b = [more_columns(values, w_o, half, third)]
    came, parts_b = lax.optimization_barrier((flip(rows_a, "dp", outer[0]), parts_b))
    held_a = jnp.concatenate([rows_a, came], axis=0)
    values, held_a = lax.optimization_barrier((values, held_a))
    parts_b.append(more_columns(values, w_o, half + third, third))
    for bit in outer[1:]:
        held_a = jnp.concatenate([held_a, flip(held_a, "dp", bit)], axis=0)
    values, parts_b, held_a = lax.optimization_barrier((values, parts_b, held_a))
    x_a = flip(held_a, "dp", inner_x)
    y_a = flip(held_a, "dp", inner_y)
    parts_b.append(more_columns(values, w_o, half + 2 * third, half - 2 * third))
    parts_b, x_a, y_a = lax.optimization_barrier((parts_b, x_a, y_a))

    hidden_b = tokens[:, half:] + head_sums(jnp.concatenate(parts_b, axis=1))
    squares = jnp.sum(hidden_a * hidden_a, axis=1, keepdims=True) + jnp.sum(
        hidden_b * hidden_b, axis=1, keepdims=True
    )
    factor = lax.rsqrt(squares / width + norm_eps)
    expert_ids = jnp.arange(replicas, dtype=jnp.int32)
    matches = experts[:, :, None] == expert_ids[None, None, :]
    gate_sum = jnp.sum(jnp.where(matches, gate_weights[:, :, None], 0.0), axis=1)
    terms = three_terms(gate_sum) + three_terms(factor)
    terms.append(jnp.zeros((tokens.shape[0], GATE_COLS - 3 * replicas - 3), jnp.bfloat16))
    rows_b = jnp.concatenate([narrow(hidden_b * norm_gain[None, half:])] + terms, axis=1)
    columns = jnp.arange(GATE_COLS, dtype=jnp.int32)
    gate_mask = (columns < 3 * replicas) & (columns % replicas == own_replica)
    factor_mask = (columns >= 3 * replicas) & (columns < 3 * replicas + 3)
    mask = jnp.stack([gate_mask, factor_mask]).astype(jnp.float32)
    corner_a = flip(y_a, "dp", inner_x)
    rows_b, mask = lax.optimization_barrier((rows_b, mask))
    came = flip(rows_b, "dp", outer[0])
    gate_held, up_held, down_held, mask = hold_weights(mask, w_gate, w_up, w_down)
    came, corner_a, mask = lax.optimization_barrier((came, corner_a, mask))
    held_b = jnp.concatenate([rows_b, came], axis=0)
    for bit in outer[1:]:
        held_b = jnp.concatenate([held_b, flip(held_b, "dp", bit)], axis=0)
    sets_a = all_sets((held_a, x_a, y_a, corner_a))
    x_b = flip(held_b, "dp", inner_x)
    y_b = flip(held_b, "dp", inner_y)
    sums = experts_first(sets_a, w_gate, w_up)
    x_b, y_b, sums = lax.optimization_barrier((x_b, y_b, sums))
    sets_b = all_sets((held_b, x_b, y_b, flip(x_b, "dp", inner_y)))
    near, far, rest = experts_second(sets_b, mask, sums, gate_held, up_held, down_held)
    mixture = scatter_sums((near, far), experts_rest(rest, down_held))
    hidden = jnp.concatenate([hidden_a, hidden_b], axis=1)
    layer_out = (hidden + mixture).astype(jnp.bfloat16)
    return (layer_out, arrivals)


def solution(mesh):
    in_specs = (
        P(("dp", "ep"), None),
        P("dp", "ep"),
        P("dp", None),
        P("dp"),
        P(),
        P("ep", None, None),
        P("ep", None),
        P(),
        P(("dp", "ep"), None),
        P(("dp", "ep"), None),
        P("dp", None, "ep"),
        P("dp", None, "ep"),
        P("dp", "ep", None),
    )
    out_specs = (P(("dp", "ep"), None), P("dp", None))
    return jax.shard_map(
        per_device, mesh=mesh, in_specs=in_specs, out_specs=out_specs, check_vma=False
    )
```

```python
import functools

import jax
import jax.numpy as jnp
from jax import lax
from jax.experimental import pallas as pl
from jax.experimental.pallas import tpu as pltpu
from jax.sharding import PartitionSpec as P

LAT = 512
KV = 576
V_DIM = 128
MOVE_MAX = 4
CTX = 64
GATE_COLS = 128


score_scale = 192.0 ** (-0.5)
norm_eps = 1e-06


def flip(x, axis, bit):
    pairs = [(i, i ^ bit) for i in range(lax.axis_size(axis))]
    return lax.ppermute(x, axis, pairs)


def bits_of(axis):
    size = lax.axis_size(axis)
    return [1 << b for b in range(size.bit_length() - 1)]


CHUNKS = 4
OUTER_FIRST = 0.125
IN_FLIGHT = 6 << 20


def vmem_spec():
    return pl.BlockSpec(memory_space=pltpu.VMEM)


def hbm_spec():
    return pl.BlockSpec(memory_space=pltpu.HBM)


def span(n, size):
    return pl.ds(pl.multiple_of(n * size, size), size)


def attention_kernel(
    moved, lengths, queries, cached, arrived, w_uv, w_o, part, values,
    keys, context, uv_buf, o_buf, uv_sems, o_sems,
):
    requests, heads, _ = queries.shape
    latent, dim = w_uv.shape[1:]
    groups = uv_sems.shape[0]
    step = heads // groups
    chunks, depth, width = o_buf.shape

    def copy_uv(g):
        own = pl.ds(g * step, step)
        return pltpu.make_async_copy(w_uv.at[own], uv_buf.at[own], uv_sems.at[g])

    def copy_o(n):
        rows = pl.ds(n * depth, depth)
        return pltpu.make_async_copy(w_o.at[rows, pl.ds(0, width)], o_buf.at[n], o_sems.at[n])

    for g in range(groups):
        copy_uv(g).start()
    ahead = min(chunks, max(2, 2 * IN_FLIGHT // (2 * depth * width)))
    for n in range(ahead):
        copy_o(n).start()
    for i in range(requests):
        row = moved[i]
        keys[i] = jnp.where(row >= 0, arrived[jnp.maximum(row, 0)], cached[i])
    scores, limits = [], []
    for i in range(requests):
        score = lax.dot_general(
            queries[i], keys[i], (((1,), (1,)), ((), ())), preferred_element_type=jnp.float32
        )
        scores.append(score)
        limits.append(jnp.full(score.shape, lengths[i], jnp.int32))
    scores = jnp.concatenate(scores, axis=0) * score_scale
    in_range = lax.broadcasted_iota(jnp.int32, scores.shape, 1) < jnp.concatenate(limits, axis=0)
    scores = jnp.where(in_range, scores, -jnp.inf)
    row_max = jnp.max(scores, axis=1, keepdims=True)
    weights = jnp.where(in_range, jnp.exp(scores - row_max), 0.0)
    probs = (weights / jnp.sum(weights, axis=1, keepdims=True)).astype(jnp.bfloat16)
    for i in range(requests):
        context[:, i, :] = jnp.dot(
            probs[i * heads : (i + 1) * heads],
            keys[i, :, :latent],
            preferred_element_type=jnp.float32,
        )
    for g in range(groups):
        copy_uv(g).wait()
        for h in range(g * step, (g + 1) * step):
            values[:, h * dim : (h + 1) * dim] = jnp.dot(
                context[h].astype(jnp.bfloat16), uv_buf[h], preferred_element_type=jnp.float32
            ).astype(jnp.bfloat16)
    for n in range(chunks):
        copy_o(n).wait()
        if n + ahead < chunks:
            copy_o(n + ahead).start()
        product = jnp.dot(
            values[:, n * depth : (n + 1) * depth], o_buf[n], preferred_element_type=jnp.float32
        )
        if n == 0:
            part[...] = product
        else:
            part[...] += product


def attention_and_first(moved, lengths, queries, cached, arrived, w_uv, w_o, width):
    requests, heads, key_width = queries.shape
    latent = w_uv.shape[1]
    depth = w_o.shape[0]
    chunks = 8
    groups = 4 if heads % 4 == 0 else 1
    smem = pl.BlockSpec(memory_space=pltpu.SMEM)
    return pl.pallas_call(
        attention_kernel,
        out_shape=(
            jax.ShapeDtypeStruct((requests, width), jnp.float32),
            jax.ShapeDtypeStruct((requests, depth), jnp.bfloat16),
        ),
        in_specs=[smem, smem] + [vmem_spec()] * 3 + [hbm_spec()] * 2,
        out_specs=(vmem_spec(), vmem_spec()),
        scratch_shapes=[
            pltpu.VMEM(cached.shape, jnp.bfloat16),
            pltpu.VMEM((heads, requests, latent), jnp.float32),
            pltpu.VMEM(w_uv.shape, jnp.bfloat16),
            pltpu.VMEM((chunks, depth // chunks, width), jnp.bfloat16),
            pltpu.SemaphoreType.DMA((groups,)),
            pltpu.SemaphoreType.DMA((chunks,)),
        ],
        compiler_params=pltpu.CompilerParams(vmem_limit_bytes=48 << 20),
        cost_estimate=pl.CostEstimate(
            flops=2 * requests * depth * (width + latent),
            bytes_accessed=2 * depth * (width + latent),
            transcendentals=requests * heads * CTX,
        ),
        name="attention_and_first",
    )(moved, lengths, queries, cached, arrived, w_uv, w_o)


def columns_kernel(start, values, w_o, part, o_buf, o_sems):
    chunks, depth, width = o_buf.shape

    def copy_o(n):
        rows = pl.ds(n * depth, depth)
        return pltpu.make_async_copy(w_o.at[rows, pl.ds(start, width)], o_buf.at[n], o_sems.at[n])

    ahead = min(chunks, max(2, IN_FLIGHT // (2 * depth * width)))
    for n in range(ahead):
        copy_o(n).start()
    for n in range(chunks):
        copy_o(n).wait()
        if n + ahead < chunks:
            copy_o(n + ahead).start()
        product = jnp.dot(
            values[:, n * depth : (n + 1) * depth], o_buf[n], preferred_element_type=jnp.float32
        )
        if n == 0:
            part[...] = product
        else:
            part[...] += product


def more_columns(values, w_o, start, width):
    rows, depth = values.shape
    chunks = 8
    return pl.pallas_call(
        functools.partial(columns_kernel, start),
        out_shape=jax.ShapeDtypeStruct((rows, width), jnp.float32),
        in_specs=[vmem_spec(), hbm_spec()],
        out_specs=vmem_spec(),
        scratch_shapes=[
            pltpu.VMEM((chunks, depth // chunks, width), jnp.bfloat16),
            pltpu.SemaphoreType.DMA((chunks,)),
        ],
        compiler_params=pltpu.CompilerParams(vmem_limit_bytes=24 << 20),
        cost_estimate=pl.CostEstimate(
            flops=2 * rows * depth * width, bytes_accessed=2 * depth * width, transcendentals=0
        ),
        name="more_columns",
    )(values, w_o)


def first_kernel(piece_count, *refs):
    pieces, refs = refs[:piece_count], refs[piece_count:]
    w_gate, w_up, gate_acc, up_acc, gate_buf, up_buf, sems = refs
    chunks, size, _ = gate_buf.shape

    def copies_in(n):
        return (
            pltpu.make_async_copy(w_gate.at[0, span(n, size)], gate_buf.at[n], sems.at[0, n]),
            pltpu.make_async_copy(w_up.at[0, span(n, size)], up_buf.at[n], sems.at[1, n]),
        )

    for n in range(chunks):
        for copy in copies_in(n):
            copy.start()
    for n in range(chunks):
        columns = slice(n * size, (n + 1) * size)
        rows = jnp.concatenate([ref[:, columns] for ref in pieces], axis=0)
        for copy in copies_in(n):
            copy.wait()
        gate_part = jnp.dot(rows, gate_buf[n], preferred_element_type=jnp.float32)
        up_part = jnp.dot(rows, up_buf[n], preferred_element_type=jnp.float32)
        if n == 0:
            gate_acc[...] = gate_part
            up_acc[...] = up_part
        else:
            gate_acc[...] += gate_part
            up_acc[...] += up_part


def experts_first(sets, w_gate, w_up):
    width, hidden_units = w_gate.shape[1:]
    size = width // CHUNKS
    flat = [piece for pieces in sets for piece in pieces]
    rows = sum(piece.shape[0] for piece in flat)
    sums = jax.ShapeDtypeStruct((rows, hidden_units), jnp.float32)
    return pl.pallas_call(
        functools.partial(first_kernel, len(flat)),
        out_shape=(sums, sums),
        in_specs=[vmem_spec()] * len(flat) + [hbm_spec()] * 2,
        out_specs=(vmem_spec(), vmem_spec()),
        scratch_shapes=[
            pltpu.VMEM((CHUNKS // 2, size, hidden_units), jnp.bfloat16),
            pltpu.VMEM((CHUNKS // 2, size, hidden_units), jnp.bfloat16),
            pltpu.SemaphoreType.DMA((2, CHUNKS // 2)),
        ],
        compiler_params=pltpu.CompilerParams(vmem_limit_bytes=32 << 20),
        cost_estimate=pl.CostEstimate(
            flops=2 * rows * width * hidden_units,
            bytes_accessed=2 * width * hidden_units + rows * width,
            transcendentals=0,
        ),
        name="experts_first",
    )(*flat, w_gate, w_up)


def hold_kernel(after, w_gate, w_up, w_down, gate, up, down, done, sems):
    half = gate.shape[0]
    parts = sems.shape[1]

    def copies(n):
        size = half // parts
        rows = pl.ds(n * size, size)
        later = pl.ds(half + n * size, size)
        units = pl.ds(n * (down.shape[0] // parts), down.shape[0] // parts)
        return (
            pltpu.make_async_copy(w_gate.at[0, later], gate.at[rows], sems.at[0, n]),
            pltpu.make_async_copy(w_up.at[0, later], up.at[rows], sems.at[1, n]),
            pltpu.make_async_copy(w_down.at[0, units], down.at[units], sems.at[2, n]),
        )

    for n in range(parts):
        for copy in copies(n):
            copy.start()
    done[...] = after[...]
    for n in range(parts):
        for copy in copies(n):
            copy.wait()


def hold_weights(after, w_gate, w_up, w_down):
    width, hidden_units = w_gate.shape[1:]
    half = width // 2
    return pl.pallas_call(
        hold_kernel,
        out_shape=(
            pltpu.VMEM((half, hidden_units), jnp.bfloat16),
            pltpu.VMEM((half, hidden_units), jnp.bfloat16),
            pltpu.VMEM((hidden_units, width), jnp.bfloat16),
            jax.ShapeDtypeStruct(after.shape, after.dtype),
        ),
        in_specs=[vmem_spec()] + [hbm_spec()] * 3,
        out_specs=(vmem_spec(),) * 4,
        scratch_shapes=[pltpu.SemaphoreType.DMA((3, 2))],
        compiler_params=pltpu.CompilerParams(vmem_limit_bytes=4 << 20),
        cost_estimate=pl.CostEstimate(
            flops=0, bytes_accessed=4 * width * hidden_units, transcendentals=0
        ),
        name="hold_weights",
    )(after, w_gate, w_up, w_down)


def held(array):
    return pltpu.with_memory_space_constraint(array, pltpu.VMEM)


def second_kernel(set_count, *refs):
    pieces, refs = refs[: 4 * set_count], refs[4 * set_count :]
    mask, gate_first, up_first, w_gate, w_up, w_down = refs[:6]
    near, far, rest, gate_acc, up_acc, act = refs[6:]
    half = w_gate.shape[0]
    size = half // 2
    line = near.shape[0] * 2 // set_count
    terms = jnp.concatenate([ref[:, half:] for ref in pieces], axis=0).astype(jnp.float32)
    gates = jnp.sum(terms * mask[0:1], axis=1, keepdims=True)
    factors = jnp.sum(terms * mask[1:2], axis=1, keepdims=True)
    for n in range(2):
        depth = slice(n * size, (n + 1) * size)
        rows = jnp.concatenate([ref[:, depth] for ref in pieces], axis=0)
        before = (gate_first, up_first) if n == 0 else (gate_acc, up_acc)
        gate_acc[...] = before[0][...] + jnp.dot(
            rows, w_gate[depth], preferred_element_type=jnp.float32
        )
        up_acc[...] = before[1][...] + jnp.dot(
            rows, w_up[depth], preferred_element_type=jnp.float32
        )
    gated = gate_acc[...] * factors
    raised = up_acc[...] * factors
    act[...] = (gated / (1.0 + jnp.exp(-gated)) * raised * gates).astype(jnp.bfloat16)
    corners = []
    for n in range(set_count):
        rest[n * 3 * line : (n + 1) * 3 * line] = act[n * 4 * line : (n * 4 + 3) * line]
        corners.append(act[(n * 4 + 3) * line : (n + 1) * 4 * line])
    corner = jnp.concatenate(corners, axis=0)
    mine = near.shape[0]

    @pl.loop(0, CHUNKS)
    def _(n):
        columns = span(n, size)
        product = jnp.dot(corner, w_down[:, columns], preferred_element_type=jnp.float32)
        near[:, columns] = product[:mine].astype(jnp.bfloat16)
        far[:, columns] = product[mine:].astype(jnp.bfloat16)


def experts_second(sets, mask, sums, w_gate, w_up, w_down):
    hidden_units, width = w_down.shape
    rows = sums[0].shape[0]
    flat = [piece for pieces in sets for piece in pieces]
    corner = jax.ShapeDtypeStruct((rows // 8, width), jnp.bfloat16)
    return pl.pallas_call(
        functools.partial(second_kernel, len(sets)),
        out_shape=(
            corner,
            corner,
            jax.ShapeDtypeStruct((rows // 4 * 3, hidden_units), jnp.bfloat16),
        ),
        in_specs=[vmem_spec()] * (len(flat) + 6),
        out_specs=(vmem_spec(),) * 3,
        scratch_shapes=[
            pltpu.VMEM((rows, hidden_units), jnp.float32),
            pltpu.VMEM((rows, hidden_units), jnp.float32),
            pltpu.VMEM((rows, hidden_units), jnp.bfloat16),
        ],
        compiler_params=pltpu.CompilerParams(vmem_limit_bytes=24 << 20),
        cost_estimate=pl.CostEstimate(
            flops=3 * rows * width * hidden_units,
            bytes_accessed=2 * rows * width,
            transcendentals=rows * hidden_units,
        ),
        name="experts_second",
    )(*flat, mask, *sums, held(w_gate), held(w_up), held(w_down))


def rest_kernel(rest, w_down, near, far):
    size = w_down.shape[1] // CHUNKS
    mine = near.shape[0]

    @pl.loop(0, CHUNKS)
    def _(n):
        columns = span(n, size)
        product = jnp.dot(rest[...], w_down[:, columns], preferred_element_type=jnp.float32)
        near[:, columns] = product[:mine].astype(jnp.bfloat16)
        far[:, columns] = product[mine:].astype(jnp.bfloat16)


def experts_rest(rest, w_down):
    rows, hidden_units = rest.shape
    width = w_down.shape[1]
    outs = jax.ShapeDtypeStruct((rows // 2, width), jnp.bfloat16)
    return pl.pallas_call(
        rest_kernel,
        out_shape=(outs, outs),
        in_specs=[vmem_spec()] * 2,
        out_specs=(vmem_spec(),) * 2,
        compiler_params=pltpu.CompilerParams(vmem_limit_bytes=24 << 20),
        cost_estimate=pl.CostEstimate(
            flops=2 * rows * width * hidden_units, bytes_accessed=2 * rows * width, transcendentals=0
        ),
        name="experts_rest",
    )(rest, held(w_down))


def moves(destination, replica_rows):
    slots = destination.shape[0]
    replicas = slots // replica_rows
    ids = jnp.arange(slots, dtype=jnp.int32)
    home = ids // replica_rows
    leaving = destination // replica_rows != home
    earlier = (home[:, None] == home[None, :]) & (ids[:, None] < ids[None, :])
    rank = jnp.sum(jnp.where(earlier & leaving[:, None], 1, 0), axis=0)
    box = jnp.where(leaving, home * MOVE_MAX + rank, -1)
    boxes = jnp.arange(replicas * MOVE_MAX, dtype=jnp.int32)
    to_box = (boxes[:, None] == box[None, :]).astype(jnp.bfloat16)
    lands = (ids[:, None] == destination[None, :]).astype(jnp.bfloat16)
    target = jnp.dot(to_box, lands, preferred_element_type=jnp.float32).astype(jnp.bfloat16)
    picker = lax.dot_general(
        target, to_box, (((1,), (1,)), ((), ())), preferred_element_type=jnp.float32
    ).astype(jnp.bfloat16)
    return picker


def migrate(packing, picker, latent_cache):
    replicas = lax.axis_size("dp")
    ep_count = lax.axis_size("ep")
    width = latent_cache.shape[1] // ep_count
    share = width // replicas
    own = lax.dynamic_slice_in_dim(latent_cache, lax.axis_index("ep") * width, width, axis=1)
    outbox = jnp.dot(packing, own, preferred_element_type=jnp.float32).astype(jnp.bfloat16)
    outbox = outbox.reshape(MOVE_MAX, replicas, share).transpose(1, 0, 2)
    met = lax.all_to_all(outbox, "dp", split_axis=0, concat_axis=0)
    sorted_rows = jnp.dot(
        picker, met.reshape(replicas * MOVE_MAX, share), preferred_element_type=jnp.float32
    ).astype(jnp.bfloat16)
    taken = lax.all_to_all(
        sorted_rows.reshape(replicas, MOVE_MAX, share), "dp", split_axis=0, concat_axis=0
    )
    part = taken.transpose(1, 0, 2).reshape(MOVE_MAX, width)
    return lax.all_gather(part, "ep", axis=1, tiled=True)


def all_sets(pieces):
    sets = [pieces]
    for bit in bits_of("ep"):
        sets = sets + [tuple(flip(piece, "ep", bit) for piece in one) for one in sets]
    return sets


def dp_bits():
    inner_x, inner_y, *outer = bits_of("dp")
    return inner_x, inner_y, outer[::-1]


def plus(*terms):
    return sum(term.astype(jnp.float32) for term in terms)


def narrow(x):
    return x.astype(jnp.bfloat16)


def ep_sums(near, far):
    bits = bits_of("ep")[::-1]
    for bit in bits:
        came = flip(far, "ep", bit)
        if bit != bits[-1]:
            near, far = jnp.split(narrow(plus(near, came)), 2, axis=0)
    return near, came


def outer_sums(lines, bits):
    for bit in bits:
        mine, other = jnp.split(lines, 2, axis=1)
        lines = mine + plus(flip(narrow(other), "dp", bit))
    return lines


def scatter_sums(corner, rest):
    inner_x, inner_y, outer = dp_bits()
    longest, *nearer = outer
    nearer = nearer[::-1]
    width = corner[0].shape[1]
    main = width - int(width * OUTER_FIRST) // 128 * 128
    half = main // 2 // 128 * 128
    corner = ep_sums(*corner)
    diagonal = narrow(plus(*(term[:, :main] for term in corner)))
    low = flip(diagonal[:, :half], "dp", inner_x)
    high = flip(diagonal[:, half:], "dp", inner_y)
    rest = [jnp.split(term, 3, axis=0) for term in ep_sums(*rest)]

    lines = [plus(*(term[n][:, main:] for term in rest)) for n in range(3)]
    lines.append(plus(*(term[:, main:] for term in corner)))
    lines = outer_sums(jnp.stack(lines), nearer)

    own, to_x, to_y = (plus(*(term[n][:, :main] for term in rest)) for n in range(3))
    to_x = narrow(jnp.concatenate([to_x[:, :half], to_x[:, half:] + plus(high)], axis=1))
    to_y = narrow(jnp.concatenate([to_y[:, :half] + plus(low), to_y[:, half:]], axis=1))
    from_x = flip(to_x, "dp", inner_x)
    from_y = flip(to_y, "dp", inner_y)
    far = flip(narrow(lines[3]), "dp", inner_x)
    from_x, from_y, far = lax.optimization_barrier((from_x, from_y, far))
    first = outer_sums(plus(own, from_x, from_y)[None], nearer)[0]

    own, to_x, to_y, _ = lines
    to_y = to_y + plus(far)
    from_x = flip(narrow(to_x), "dp", inner_x)
    from_y = flip(narrow(to_y), "dp", inner_y)
    last = own + plus(from_x, from_y)
    return outer_sums(jnp.concatenate([first, last], axis=1)[None], [longest])[0]


def head_sums(part):
    if lax.axis_size("ep") != 2:
        return lax.psum_scatter(part, "ep", scatter_dimension=0, tiled=True)
    rows = part.shape[0] // 2
    own = lax.axis_index("ep")
    mine = lax.dynamic_slice_in_dim(part, own * rows, rows)
    other = lax.dynamic_slice_in_dim(part, (1 - own) * rows, rows)
    return mine + flip(other, "ep", 1)


def three_terms(x):
    terms = []
    for _ in range(3):
        term = lax.reduce_precision(x, 8, 7)
        terms.append(narrow(term))
        x = x - term
    return terms


def per_device(
    residual,
    queries,
    latent_cache,
    lengths,
    destination,
    w_uv,
    w_o,
    norm_gain,
    experts,
    gate_weights,
    w_gate,
    w_up,
    w_down,
):
    w_uv, w_o, w_gate, w_up, w_down = (
        pltpu.with_memory_space_constraint(w, pltpu.HBM) for w in (w_uv, w_o, w_gate, w_up, w_down)
    )
    replica_rows = latent_cache.shape[0]
    replicas = destination.shape[0] // replica_rows
    own_replica = lax.axis_index("dp")
    picker = moves(destination, replica_rows)
    own_slots = lax.dynamic_slice_in_dim(destination, own_replica * replica_rows, replica_rows)
    leaving = own_slots // replica_rows != own_replica
    places = jnp.arange(replica_rows, dtype=jnp.int32)
    earlier = (places[:, None] < places[None, :]) & leaving[:, None]
    rank = jnp.sum(earlier.astype(jnp.int32), axis=0)
    box_ids = jnp.arange(MOVE_MAX, dtype=jnp.int32)
    packing = narrow((rank[None, :] == box_ids[:, None]) & leaving[None, :])
    arrivals = migrate(packing, picker, latent_cache)
    boxes = jnp.arange(1, MOVE_MAX + 1, dtype=jnp.float32)[:, None]
    moved = jnp.sum(packing.astype(jnp.float32) * boxes, axis=0).astype(jnp.int32) - 1
    heads_dev = w_uv.shape[0]
    query_rows = queries.reshape(replica_rows, heads_dev, KV)
    cached = latent_cache.reshape(replica_rows, CTX, KV)
    arrived = arrivals.reshape(MOVE_MAX, CTX, KV)
    width = residual.shape[1]
    half = width // 2
    tokens = residual.astype(jnp.float32)

    part, values = attention_and_first(
        moved, lengths, query_rows, cached, arrived, w_uv, w_o, half
    )
    hidden_a = tokens[:, :half] + head_sums(part)
    rows_a = narrow(hidden_a * norm_gain[None, :half])
    values, rows_a = lax.optimization_barrier((values, rows_a))
    inner_x, inner_y, outer = dp_bits()
    third = half * 2 // 7 // 128 * 128
    parts_b = [more_columns(values, w_o, half, third)]
    came, parts_b = lax.optimization_barrier((flip(rows_a, "dp", outer[0]), parts_b))
    held_a = jnp.concatenate([rows_a, came], axis=0)
    values, held_a = lax.optimization_barrier((values, held_a))
    parts_b.append(more_columns(values, w_o, half + third, third))
    for bit in outer[1:]:
        held_a = jnp.concatenate([held_a, flip(held_a, "dp", bit)], axis=0)
    values, parts_b, held_a = lax.optimization_barrier((values, parts_b, held_a))
    x_a = flip(held_a, "dp", inner_x)
    y_a = flip(held_a, "dp", inner_y)
    parts_b.append(more_columns(values, w_o, half + 2 * third, half - 2 * third))
    parts_b, x_a, y_a = lax.optimization_barrier((parts_b, x_a, y_a))

    hidden_b = tokens[:, half:] + head_sums(jnp.concatenate(parts_b, axis=1))
    squares = jnp.sum(hidden_a * hidden_a, axis=1, keepdims=True) + jnp.sum(
        hidden_b * hidden_b, axis=1, keepdims=True
    )
    factor = lax.rsqrt(squares / width + norm_eps)
    expert_ids = jnp.arange(replicas, dtype=jnp.int32)
    matches = experts[:, :, None] == expert_ids[None, None, :]
    gate_sum = jnp.sum(jnp.where(matches, gate_weights[:, :, None], 0.0), axis=1)
    terms = three_terms(gate_sum) + three_terms(factor)
    terms.append(jnp.zeros((tokens.shape[0], GATE_COLS - 3 * replicas - 3), jnp.bfloat16))
    rows_b = jnp.concatenate([narrow(hidden_b * norm_gain[None, half:])] + terms, axis=1)
    columns = jnp.arange(GATE_COLS, dtype=jnp.int32)
    gate_mask = (columns < 3 * replicas) & (columns % replicas == own_replica)
    factor_mask = (columns >= 3 * replicas) & (columns < 3 * replicas + 3)
    mask = jnp.stack([gate_mask, factor_mask]).astype(jnp.float32)
    corner_a = flip(y_a, "dp", inner_x)
    rows_b, mask = lax.optimization_barrier((rows_b, mask))
    came = flip(rows_b, "dp", outer[0])
    gate_held, up_held, down_held, mask = hold_weights(mask, w_gate, w_up, w_down)
    came, corner_a, mask = lax.optimization_barrier((came, corner_a, mask))
    held_b = jnp.concatenate([rows_b, came], axis=0)
    for bit in outer[1:]:
        held_b = jnp.concatenate([held_b, flip(held_b, "dp", bit)], axis=0)
    sets_a = all_sets((held_a, x_a, y_a, corner_a))
    x_b = flip(held_b, "dp", inner_x)
    y_b = flip(held_b, "dp", inner_y)
    sums = experts_first(sets_a, w_gate, w_up)
    x_b, y_b, sums = lax.optimization_barrier((x_b, y_b, sums))
    sets_b = all_sets((held_b, x_b, y_b, flip(x_b, "dp", inner_y)))
    near, far, rest = experts_second(sets_b, mask, sums, gate_held, up_held, down_held)
    mixture = scatter_sums((near, far), experts_rest(rest, down_held))
    hidden = jnp.concatenate([hidden_a, hidden_b], axis=1)
    layer_out = (hidden + mixture).astype(jnp.bfloat16)
    return (layer_out, arrivals)


def solution(mesh):
    in_specs = (
        P(("dp", "ep"), None),
        P("dp", "ep"),
        P("dp", None),
        P("dp"),
        P(),
        P("ep", None, None),
        P("ep", None),
        P(),
        P(("dp", "ep"), None),
        P(("dp", "ep"), None),
        P("dp", None, "ep"),
        P("dp", None, "ep"),
        P("dp", "ep", None),
    )
    out_specs = (P(("dp", "ep"), None), P("dp", None))
    return jax.shard_map(
        per_device, mesh=mesh, in_specs=in_specs, out_specs=out_specs, check_vma=False
    )
```
